32 devices in a mesh: space: 8 (over z, y), dp: 4 (over x, core).
Axes of the slice: x: 2, y: 2, z: 4, core: 2. Of those that a mesh axis runs over, the one named last changes fastest.
Arguments:
- activations: bfloat16 [4, 64, 16, 16, 256], P('dp', 'space'), may hold values from -6 to 6
- cotangent: bfloat16 [4, 64, 16, 16, 256], P('dp', 'space'), may hold values from -6 to 6
- tile_count: int32 [8], P('space'), may hold values from 1 to 8, as said below
- neighbours: int32 [64, 8], P('space'), may hold values from -1 to 63, as said below
- conv_kernel: float32 [7, 7, 256], replicated, may hold values from -0.875 to 0.875
- conv_bias: float32 [256], replicated, may hold values from -3 to 3
- norm_gain: float32 [256], replicated, may hold values from 0.1 to 1.9
- norm_bias: float32 [256], replicated, may hold values from -3 to 3
- proj_in: bfloat16 [256, 1024], replicated, may hold values from -0.375 to 0.375
- bias_in: float32 [1024], replicated, may hold values from -3 to 3
- proj_out: bfloat16 [1024, 256], replicated, may hold values from -0.1875 to 0.1875
- bias_out: float32 [256], replicated, may hold values from -3 to 3
- layer_scale: float32 [256], replicated, may hold values from 0.3 to 3
Outputs:
- out_tiles: bfloat16 [4, 64, 16, 16, 256], P('dp', 'space')
- grad_tiles: bfloat16 [4, 64, 16, 16, 256], P('dp', 'space')
- grad_conv_kernel: float32 [7, 7, 256], replicated
- grad_conv_bias: float32 [256], replicated
- grad_norm_gain: float32 [256], replicated
- grad_norm_bias: float32 [256], replicated
- grad_proj_in: float32 [256, 1024], replicated
- grad_bias_in: float32 [1024], replicated
- grad_proj_out: float32 [1024, 256], replicated
- grad_bias_out: float32 [256], replicated
- grad_layer_scale: float32 [256], replicated
The draws below stay inside these ranges and needn't reach their ends.
Inputs may be any that keep to these rules, and one draw needn't show every extreme that they name: `tile_count`: each tile column has 1 to 8 ocean tiles; its live slots come first in its block, and the last tile column is all ocean. Tile rows do not wrap, tile columns wrap around. N and S neighbours are slots of the same column, W, NW, SW of the column to the left and E, NE, SE of the column to the right; a neighbour that is land or beyond the band, and every entry of a slot that is not live, is -1. Named slots are live.
All inputs are finite; a program needn't handle non-finite values.
Results may differ from the reference program's by a relative error of at most 0.0085.
Values may be sent and summed in bfloat16 or wider, within the bound.
No kernel may reach another device: no remote copies, remote signals or barrier semaphores. Data moves between devices by JAX's collectives and lax.ppermute only.
A program may use at most 64 MiB of HBM per device.

```python
import math
import jax
import jax.numpy as jnp
from jax import lax

C = 256
HID = 1024
TILE = 16
SLOTS = 8
BATCH = 4
TILES = 64
CELLS = 65536
N_SPACE = 8


DIRECTIONS = ((-1, 0), (1, 0), (0, -1), (0, 1), (-1, -1), (-1, 1), (1, -1), (1, 1))


def ocean_layout(key):
    land_draw = jax.random.randint(jax.random.fold_in(key, 11), (SLOTS, N_SPACE), 0, 5)
    row_pos = jnp.arange(SLOTS, dtype=jnp.int32)
    col_pos = jnp.arange(N_SPACE, dtype=jnp.int32)
    keep_row = jax.random.randint(jax.random.fold_in(key, 12), (N_SPACE,), 0, SLOTS)
    full_col = N_SPACE - 1
    ocean = (land_draw < 3) | (row_pos[:, None] == keep_row[None, :]) | (col_pos[None, :] == full_col)
    ocean_int = ocean.astype(jnp.int32)
    counts = jnp.sum(ocean_int, axis=0).astype(jnp.int32)
    ranks = (jnp.cumsum(ocean_int, axis=0) - 1).astype(jnp.int32)
    matches = (ocean_int[None, :, :] == 1) & (ranks[None, :, :] == row_pos[:, None, None])
    slot_row = jnp.sum(jnp.where(matches, row_pos[None, :, None], 0), axis=1).astype(jnp.int32)
    slot_live = row_pos[:, None] < counts[None, :]
    link_list = []
    for row_step, col_step in DIRECTIONS:
        target_row = slot_row + row_step
        target_col = jnp.broadcast_to((col_pos[None, :] + col_step) % N_SPACE, target_row.shape).astype(jnp.int32)
        inside = (target_row >= 0) & (target_row < SLOTS)
        safe_row = jnp.clip(target_row, 0, SLOTS - 1).astype(jnp.int32)
        is_ocean = ocean_int[safe_row, target_col] == 1
        global_id = target_col * SLOTS + ranks[safe_row, target_col]
        link_list.append(jnp.where(slot_live & inside & is_ocean, global_id, -1).astype(jnp.int32))
    link_table = jnp.stack(link_list, axis=-1)
    return (counts, jnp.transpose(link_table, (1, 0, 2)).reshape(N_SPACE * SLOTS, 8))


def draw_tile_count(key, part):
    counts, link_table = ocean_layout(key)
    return counts.astype(jnp.int32)


def draw_neighbours(key, part):
    counts, link_table = ocean_layout(key)
    return link_table.astype(jnp.int32)


def block_scale(rng, shape, cuts, smallest, high):
    def one(dim, shards_of):
        heights = jax.random.uniform(jax.random.fold_in(jax.random.fold_in(rng, 6), dim), (shards_of,), jnp.float32, smallest / len(cuts), high / len(cuts))
        return jnp.repeat(jnp.exp(heights), shape[dim] // shards_of).reshape((-1,) + (1,) * (len(shape) - dim - 1))

    gain = one(*cuts[0])
    for cut in cuts[1:]:
        gain = gain * one(*cut)
    return gain


def gaussian(own_key, dims, scale, most, shards=(), kind=jnp.bfloat16):
    gain = block_scale(own_key, dims, shards, -0.22, 0.18) if shards else 1.0
    drawn = jax.random.normal(own_key, dims, jnp.float32) * scale * gain
    return jnp.minimum(jnp.maximum(drawn, -most), most).astype(kind)


def setup_inputs(seed: int = 0) -> dict:
    key_list = jax.random.split(jax.random.key(seed), 14)
    return {
        "activations": gaussian(key_list[0], (BATCH, TILES, TILE, TILE, C), 1.0, 6.0, ((0, 4), (1, 8))),
        "cotangent": gaussian(key_list[1], (BATCH, TILES, TILE, TILE, C), 1.0, 6.0, ((0, 4), (1, 8))),
        "tile_count": draw_tile_count(jax.random.fold_in(key_list[13], 71), 0),
        "neighbours": draw_neighbours(jax.random.fold_in(key_list[13], 71), 0),
        "conv_kernel": gaussian(key_list[4], (7, 7, C), 49 ** -0.5, 0.875, (), jnp.float32),
        "conv_bias": gaussian(key_list[5], (C,), 0.5, 3.0, (), jnp.float32),
        "norm_gain": jnp.clip(1.0 + 0.18 * jax.random.normal(key_list[6], (C,), jnp.float32), 0.1, 1.9),
        "norm_bias": gaussian(key_list[7], (C,), 0.5, 3.0, (), jnp.float32),
        "proj_in": gaussian(key_list[8], (C, HID), C ** -0.5, 0.375),
        "bias_in": gaussian(key_list[9], (HID,), 0.5, 3.0, (), jnp.float32),
        "proj_out": gaussian(key_list[10], (HID, C), HID ** -0.5, 0.1875),
        "bias_out": gaussian(key_list[11], (C,), 0.5, 3.0, (), jnp.float32),
        "layer_scale": jnp.clip(jnp.exp(jax.random.uniform(key_list[12], (C,), jnp.float32, math.log(0.3), math.log(3.0))), 0.3, 3.0),
    }


ROOT_TWO_PI = 0.7978845608
CUBIC_TERM = 0.044715
EPSILON = 1e-06

def gelu_pair(pre_act):
    tangent = jnp.tanh(ROOT_TWO_PI * (pre_act + CUBIC_TERM * pre_act * pre_act * pre_act))
    activated = 0.5 * pre_act * (1.0 + tangent)
    slope_vals = 0.5 * (1.0 + tangent) + 0.5 * pre_act * (1.0 - tangent * tangent) * ROOT_TWO_PI * (1.0 + 3.0 * CUBIC_TERM * pre_act * pre_act)
    return (activated, slope_vals)

def assemble(center, north_rows, south_rows, west_cols, east_cols, corner_nw, corner_ne, corner_sw, corner_se):
    top_band = jnp.concatenate([corner_nw, north_rows, corner_ne], axis=-2)
    mid_band = jnp.concatenate([west_cols, center, east_cols], axis=-2)
    low_band = jnp.concatenate([corner_sw, south_rows, corner_se], axis=-2)
    return jnp.concatenate([top_band, mid_band, low_band], axis=-3)

def tile_pieces(own_tiles, west_data, east_data, ids_row, slot_count, center):
    present = ids_row >= 0
    local_ids = jnp.where(present, ids_row % slot_count, 0).astype(jnp.int32)
    tile_edge = own_tiles.shape[1]

    def masked_piece(piece, which):
        return jnp.where(present[which], piece, jnp.zeros_like(piece))
    return assemble(center, masked_piece(own_tiles[local_ids[0], tile_edge - 3:], 0), masked_piece(own_tiles[local_ids[1], :3], 1), masked_piece(west_data[local_ids[2]], 2), masked_piece(east_data[local_ids[3]], 3), masked_piece(west_data[local_ids[4], tile_edge - 3:], 4), masked_piece(east_data[local_ids[5], tile_edge - 3:], 5), masked_piece(west_data[local_ids[6], :3], 6), masked_piece(east_data[local_ids[7], :3], 7))

def depthwise(padded, kernel, col_start, col_stop):
    tile_edge = padded.shape[-3] - 6
    conv_sum = jnp.zeros(padded.shape[:-3] + (tile_edge, col_stop - col_start, padded.shape[-1]), jnp.float32)
    for row_tap in range(7):
        for col_tap in range(7):
            window = padded[..., row_tap:row_tap + tile_edge, col_start + col_tap:col_stop + col_tap, :]
            conv_sum = conv_sum + window.astype(jnp.float32) * kernel[row_tap, col_tap]
    return conv_sum

def transposed(padded, kernel):
    tile_edge = padded.shape[-3] - 6
    conv_sum = jnp.zeros(padded.shape[:-3] + (tile_edge, tile_edge, padded.shape[-1]), jnp.float32)
    for row_tap in range(7):
        for col_tap in range(7):
            window = padded[..., 6 - row_tap:6 - row_tap + tile_edge, 6 - col_tap:6 - col_tap + tile_edge, :]
            conv_sum = conv_sum + window.astype(jnp.float32) * kernel[row_tap, col_tap]
    return conv_sum

def kernel_grad(padded, grad_vals):
    tile_edge = padded.shape[-3] - 6
    axes_all = tuple(range(grad_vals.ndim - 1))
    tap_list = []
    for row_tap in range(7):
        for col_tap in range(7):
            window = padded[..., row_tap:row_tap + tile_edge, col_tap:col_tap + tile_edge, :]
            tap_list.append(lax.optimization_barrier(jnp.sum(window.astype(jnp.float32) * grad_vals, axis=axes_all)))
    return jnp.stack(tap_list).reshape(7, 7, -1)

def reference(activations, cotangent, tile_count, neighbours, conv_kernel, conv_bias, norm_gain, norm_bias, proj_in, bias_in, proj_out, bias_out, layer_scale):
    slot_ids = jnp.arange(TILES, dtype=jnp.int32)
    live = slot_ids % SLOTS < tile_count[slot_ids // SLOTS]
    live_rows = jnp.repeat(live, TILE * TILE)[:, None]
    live_tiles = live[:, None, None, None]

    def pad_all(sample_tiles):
        west_data = sample_tiles[:, :, TILE - 3:]
        east_data = sample_tiles[:, :, :3]
        return jax.vmap(lambda ids_row, center: tile_pieces(sample_tiles, west_data, east_data, ids_row, TILES, center))(neighbours, sample_tiles)

    def one_sample(pair):
        sample_tiles, sample_grad = pair
        padded = pad_all(sample_tiles)
        conv_out = (depthwise(padded, conv_kernel, 0, TILE) + conv_bias).reshape(-1, C)
        centred = conv_out - lax.optimization_barrier(jnp.mean(conv_out, axis=1, keepdims=True))
        inv_std = lax.rsqrt(lax.optimization_barrier(jnp.mean(centred * centred, axis=1, keepdims=True)) + EPSILON)
        normed = centred * inv_std
        unit_bf = (normed * norm_gain + norm_bias).astype(jnp.bfloat16)
        pre_act = jnp.dot(unit_bf, proj_in, preferred_element_type=jnp.float32) + bias_in
        activated, slope_vals = gelu_pair(pre_act)
        act_bf = activated.astype(jnp.bfloat16)
        branch = jnp.dot(act_bf, proj_out, preferred_element_type=jnp.float32) + bias_out
        x_rows = sample_tiles.reshape(-1, C).astype(jnp.float32)
        out_rows = jnp.where(live_rows, x_rows + layer_scale * branch, 0.0).astype(jnp.bfloat16)
        dy_rows = jnp.where(live_rows, sample_grad.reshape(-1, C).astype(jnp.float32), 0.0)
        grad_branch = (dy_rows * layer_scale).astype(jnp.bfloat16)
        grad_wout = jnp.dot(act_bf.T, grad_branch, preferred_element_type=jnp.float32)
        grad_act = jnp.dot(grad_branch, proj_out.T, preferred_element_type=jnp.float32)
        grad_pre = (grad_act * slope_vals).astype(jnp.bfloat16)
        grad_win = jnp.dot(unit_bf.T, grad_pre, preferred_element_type=jnp.float32)
        grad_unit = jnp.dot(grad_pre, proj_in.T, preferred_element_type=jnp.float32)
        scaled = grad_unit * norm_gain
        grad_conv = inv_std * (scaled - lax.optimization_barrier(jnp.mean(scaled, axis=1, keepdims=True)) - normed * lax.optimization_barrier(jnp.mean(scaled * normed, axis=1, keepdims=True)))
        grad_conv_bf = grad_conv.astype(jnp.bfloat16)
        grad_conv_tiles = grad_conv_bf.reshape(TILES, TILE, TILE, C)
        grad_pad = pad_all(grad_conv_tiles)
        spread = transposed(grad_pad, conv_kernel)
        grad_x = jnp.where(live_tiles, sample_grad.astype(jnp.float32) + spread, 0.0).astype(jnp.bfloat16)
        kernel_sum = kernel_grad(padded, grad_conv_tiles.astype(jnp.float32))
        sums = (kernel_sum, lax.optimization_barrier(jnp.sum(grad_conv_bf.astype(jnp.float32), axis=0)), lax.optimization_barrier(jnp.sum(grad_unit * normed, axis=0)), lax.optimization_barrier(jnp.sum(grad_unit, axis=0)), grad_win, lax.optimization_barrier(jnp.sum(grad_pre.astype(jnp.float32), axis=0)), grad_wout, lax.optimization_barrier(jnp.sum(grad_branch.astype(jnp.float32), axis=0)), lax.optimization_barrier(jnp.sum(dy_rows * branch, axis=0)))
        return (out_rows.reshape(TILES, TILE, TILE, C), grad_x, sums)
    out_all, grad_all, sums_all = lax.map(one_sample, (activations, cotangent))
    factor = 1.0 / math.sqrt(CELLS)
    totals = [lax.optimization_barrier(jnp.sum(entry, axis=0)) * factor for entry in sums_all]
    return (out_all, grad_all, totals[0], totals[1], totals[2], totals[3], totals[4], totals[5], totals[6], totals[7], totals[8])
```

```python
import functools
import math

import jax
import jax.numpy as jnp
from jax import lax
from jax.experimental import pallas as pl
from jax.experimental.pallas import tpu as pltpu
from jax.sharding import PartitionSpec as P

ROOT_TWO_PI = 0.7978845608
CUBIC_TERM = 0.044715
EPSILON = 1e-06

F32 = jnp.float32
BF16 = jnp.bfloat16
LANES = 128
TAPS = 7
RIM = 3
AXES = ("space", "dp")
VMEM_LIMIT = 56 * 1024 * 1024


def vmem_spec():
    return pl.BlockSpec(memory_space=pltpu.VMEM)


def smem_spec():
    return pl.BlockSpec(memory_space=pltpu.SMEM)


def call(body, outs, ins, scratch=(), smem=0):
    return pl.pallas_call(
        body,
        out_shape=tuple(jax.ShapeDtypeStruct(s, d) for s, d in outs),
        in_specs=[smem_spec()] * smem + [vmem_spec()] * (len(ins) - smem),
        out_specs=tuple(vmem_spec() for _ in outs),
        scratch_shapes=list(scratch),
        compiler_params=pltpu.CompilerParams(vmem_limit_bytes=VMEM_LIMIT),
    )(*ins)


def slot_pick(nbr_ref, which):
    slots = nbr_ref.shape[0]
    row = lax.broadcasted_iota(jnp.int32, (slots, LANES), 0)
    ids = jnp.full((slots, LANES), -1, jnp.int32)
    for t in range(slots):
        ids = jnp.where(row == t, nbr_ref[t, which], ids)
    present = ids >= 0
    return jnp.where(present, lax.rem(ids, slots), 0), present


def take(v, pick):
    ids, present = pick
    return jnp.where(present, jnp.take_along_axis(v, ids, axis=0, mode="promise_in_bounds"), 0.0)


def lanes(h):
    return slice(h * LANES, (h + 1) * LANES)


def pad_col(pads, h, r, c):
    west, center, east = pads
    if c < RIM:
        return west[h, r, c * 8 : c * 8 + 8, :]
    c -= RIM
    if c < 16:
        return center[h, r, c * 8 : c * 8 + 8, :]
    c -= 16
    return east[h, r, c * 8 : c * 8 + 8, :]


def spread_taps(k_ref, k8_ref, flip):
    for h in range(2):
        for tap in range(TAPS * TAPS):
            src = TAPS * TAPS - 1 - tap if flip else tap
            k8_ref[h, tap] = jnp.broadcast_to(k_ref[src : src + 1, lanes(h)], (8, LANES))


def conv_wide(pads, k8_ref, h, r, c0, n):
    accs = [None] * n
    for i in range(TAPS):
        xs = [pad_col(pads, h, r + i, c0 + c) for c in range(n + TAPS - 1)]
        for j in range(TAPS):
            kk = k8_ref[h, i * TAPS + j]
            for c in range(n):
                term = xs[c + j] * kk
                accs[c] = term if accs[c] is None else accs[c] + term
    return accs


def conv_tall(pads, k8_ref, h, r0, rows, c0, n):
    accs = [[None] * n for _ in range(rows)]
    for j in range(TAPS):
        ks = [k8_ref[h, i * TAPS + j] for i in range(TAPS)]
        for p in range(rows + TAPS - 1):
            xs = [pad_col(pads, h, r0 + p, c0 + j + c) for c in range(n)]
            for q in range(max(0, p - TAPS + 1), min(rows, p + 1)):
                for c in range(n):
                    term = xs[c] * ks[p - q]
                    accs[q][c] = term if accs[q][c] is None else accs[q][c] + term
    return accs


def gelu_pair(pre):
    sq = pre * pre
    t = jnp.tanh(pre * (ROOT_TWO_PI + (ROOT_TWO_PI * CUBIC_TERM) * sq))
    half = 0.5 + 0.5 * t
    act = pre * half
    slope = half + act * (1.0 - t) * (ROOT_TWO_PI + (3.0 * ROOT_TWO_PI * CUBIC_TERM) * sq)
    return act, slope


def fold(v):
    return jnp.sum(v.reshape(v.shape[0] // 8, 8, v.shape[1]), axis=0)


def dot(a, b):
    return jnp.dot(a, b, preferred_element_type=F32)


def dot_t(a, b):
    return lax.dot_general(a, b, (((1,), (1,)), ((), ())), preferred_element_type=F32)


def dense_block(conv, x, dy, params, dw_ref, sums_ref):
    win, wout, bias_in, bias_out, scale, gain, shift, conv_bias = params
    hidden = win.shape[1]
    channels = win.shape[0]
    conv = conv + conv_bias[...]
    centred = conv - jnp.mean(conv, axis=1, keepdims=True)
    inv_std = lax.rsqrt(jnp.mean(centred * centred, axis=1, keepdims=True) + EPSILON)
    normed = centred * inv_std
    unit = (normed * gain[...] + shift[...]).astype(BF16)
    gb = (dy * scale[...]).astype(BF16)
    unit_t = unit.T
    gb_t = gb.T
    branch = jnp.zeros(conv.shape, F32)
    grad_unit = jnp.zeros(conv.shape, F32)
    for k in range(0, hidden, 256):
        ks = slice(k, k + 256)
        pre = dot(unit, win[:, ks]) + bias_in[:, ks]
        act, slope = gelu_pair(pre)
        act = act.astype(BF16)
        gp = (dot_t(gb, wout[ks, :]) * slope).astype(BF16)
        branch = branch + dot(act, wout[ks, :])
        grad_unit = grad_unit + dot_t(gp, win[:, ks])
        dw_ref[0:channels, ks] += dot(unit_t, gp)
        dw_ref[channels : 2 * channels, ks] += dot(gb_t, act)
        sums_ref[k // 256] += fold(gp.astype(F32))
    branch = branch + bias_out[...]
    out = x + scale[...] * branch
    scaled = grad_unit * gain[...]
    grad_conv = inv_std * (
        scaled
        - jnp.mean(scaled, axis=1, keepdims=True)
        - normed * jnp.mean(scaled * normed, axis=1, keepdims=True)
    )
    grad_conv = grad_conv.astype(BF16).astype(F32)
    nk = hidden // 256
    sums_ref[nk] += fold(gb.astype(F32))
    sums_ref[nk + 1] += fold(dy * branch)
    sums_ref[nk + 2] += fold(grad_unit * normed)
    sums_ref[nk + 3] += fold(grad_unit)
    sums_ref[nk + 4] += fold(grad_conv)
    return out, grad_conv


def rows_of(ref, r0, nr, c0, n):
    blocks = []
    for q in range(nr):
        blocks.append(jnp.concatenate([ref[h, r0 + q, c0 * 8 : (c0 + n) * 8, :] for h in range(2)], axis=1))
    return jnp.concatenate(blocks, axis=0)


def rims_of(center_ref, nbr_ref):
    north = slot_pick(nbr_ref, 0)
    south = slot_pick(nbr_ref, 1)
    for h in range(2):
        for q in range(RIM):
            for c in range(16):
                cs = slice(c * 8, c * 8 + 8)
                center_ref[h, q, cs, :] = take(center_ref[h, 16 + q, cs, :], north)
                center_ref[h, 19 + q, cs, :] = take(center_ref[h, 3 + q, cs, :], south)


def side_rim(side_ref, halo_ref, nbr_ref, straight, up, down):
    mid, top, low = (slot_pick(nbr_ref, w) for w in (straight, up, down))
    for h in range(2):
        for pair in range(24):
            v = halo_ref[pair * 16 : pair * 16 + 16, lanes(h)].astype(F32)
            for s in range(2):
                r, c = divmod(pair * 2 + s, RIM)
                cs = slice(c * 8, c * 8 + 8)
                part = v[s * 8 : s * 8 + 8]
                side_ref[h, 3 + r, cs, :] = take(part, mid)
                if r >= 13:
                    side_ref[h, r - 13, cs, :] = take(part, top)
                if r < 3:
                    side_ref[h, 19 + r, cs, :] = take(part, low)


def inner_kernel(
    nbr_ref, cnt_ref, x_ref, dy_ref, k_ref, win, wout, bias_in, bias_out, scale, gain, shift, conv_bias,
    center_ref, dyt_ref, out_ref, g_ref, dw_ref, sums_ref,
    k8_ref, conv_ref,
):
    live = cnt_ref[0]
    spread_taps(k_ref, k8_ref, False)
    dw_ref[...] = jnp.zeros(dw_ref.shape, F32)
    sums_ref[...] = jnp.zeros(sums_ref.shape, F32)

    def turn(r, carry):
        for t in range(8):
            for h in range(2):
                center_ref[h, 3 + r, pl.ds(t, 16, stride=8), :] = x_ref[t, r, :, lanes(h)].astype(F32)
                dyv = dy_ref[t, r, :, lanes(h)].astype(F32)
                dyt_ref[h, r, pl.ds(t, 16, stride=8), :] = jnp.where(t < live, dyv, 0.0)
        return carry

    lax.fori_loop(0, 16, turn, 0)
    rims_of(center_ref, nbr_ref)
    params = (win, wout, bias_in, bias_out, scale, gain, shift, conv_bias)
    nr, n, c0 = 4, 10, 3
    pads = (None, center_ref, None)

    def block(m, carry):
        r0 = m * nr

        def conv(q, carry):
            for h in range(2):
                accs = conv_wide(pads, k8_ref, h, r0 + q, c0, n)
                conv_ref[pl.ds(pl.multiple_of(q * n * 8, 8), n * 8), lanes(h)] = jnp.concatenate(accs, axis=0)
            return carry

        lax.fori_loop(0, nr, conv, 0)
        x = rows_of(center_ref, r0 + 3, nr, c0, n)
        dy = rows_of(dyt_ref, r0, nr, c0, n)
        out, g = dense_block(conv_ref[...], x, dy, params, dw_ref, sums_ref)
        for q in range(nr):
            for h in range(2):
                out_ref[h, r0 + q] = out[q * n * 8 : (q + 1) * n * 8, lanes(h)]
                g_ref[h, r0 + q] = g[q * n * 8 : (q + 1) * n * 8, lanes(h)]
        return carry

    lax.fori_loop(0, 16 // nr, block, 0)


def edge_kernel(
    nbr_ref, hw_ref, he_ref, center_ref, dyt_ref, dw_in, sums_in,
    k_ref, win, wout, bias_in, bias_out, scale, gain, shift, conv_bias,
    west_ref, east_ref, out_ref, g_ref, send_l, send_r, dw_ref, sums_ref,
    k8_ref, conv_ref,
):
    spread_taps(k_ref, k8_ref, False)
    dw_ref[...] = dw_in[...]
    sums_ref[...] = sums_in[...]
    side_rim(west_ref, hw_ref, nbr_ref, 2, 4, 6)
    side_rim(east_ref, he_ref, nbr_ref, 3, 5, 7)
    params = (win, wout, bias_in, bias_out, scale, gain, shift, conv_bias)
    pads = (west_ref, center_ref, east_ref)
    nr = 8

    def block(m, carry):
        r0 = m * nr
        for h in range(2):
            for side, c0 in enumerate((0, 13)):
                accs = conv_tall(pads, k8_ref, h, r0, nr, c0, RIM)
                for q in range(nr):
                    base = (q * 2 + side) * 24
                    conv_ref[base : base + 24, lanes(h)] = jnp.concatenate(accs[q], axis=0)
        xs, dys = [], []
        for q in range(nr):
            for c0 in (0, 13):
                xs.append(rows_of(center_ref, r0 + 3 + q, 1, c0, RIM))
                dys.append(rows_of(dyt_ref, r0 + q, 1, c0, RIM))
        x = jnp.concatenate(xs, axis=0)
        dy = jnp.concatenate(dys, axis=0)
        out, g = dense_block(conv_ref[...], x, dy, params, dw_ref, sums_ref)
        for q in range(nr):
            for h in range(2):
                out_ref[h, r0 + q] = out[q * 48 : (q + 1) * 48, lanes(h)]
                g_ref[h, r0 + q] = g[q * 48 : (q + 1) * 48, lanes(h)]
        for q in range(0, nr, 2):
            for side, send in enumerate((send_l, send_r)):
                v = jnp.concatenate(
                    [g[(q + s) * 48 + side * 24 : (q + s) * 48 + side * 24 + 24] for s in range(2)], axis=0
                )
                send[pl.ds(pl.multiple_of((r0 + q) * 24, 16), 48), :] = v.astype(BF16)
        return carry

    lax.fori_loop(0, 16 // nr, block, 0)


def full_width(inner_ref, edge_ref, h, r):
    return [edge_ref[h, r, c * 8 : c * 8 + 8, :] for c in range(3)] + [
        inner_ref[h, r, c * 8 : c * 8 + 8, :] for c in range(10)
    ] + [edge_ref[h, r, c * 8 : c * 8 + 8, :] for c in range(3, 6)]


def tap_kernel(
    center_ref, west_ref, east_ref, gi_ref, ge_ref, sums_in,
    small_ref,
    acc_ref,
):
    pads = (west_ref, center_ref, east_ref)

    def row_tap(i, carry):
        for h in range(2):

            def row(r, accs):
                g = full_width(gi_ref, ge_ref, h, r)
                xs = [pad_col(pads, h, r + i, c) for c in range(22)]
                new = []
                for j in range(TAPS):
                    terms = [xs[c + j] * g[c] for c in range(16)]
                    while len(terms) > 1:
                        terms = [a + b for a, b in zip(terms[::2], terms[1::2])]
                    new.append(accs[j] + terms[0])
                return tuple(new)

            accs = lax.fori_loop(0, 16, row, tuple(jnp.zeros((8, LANES), F32) for _ in range(TAPS)))
            for j in range(TAPS):
                acc_ref[i * TAPS + j, :, lanes(h)] = accs[j]
        return carry

    lax.fori_loop(0, TAPS, row_tap, 0)
    small_ref[...] = jnp.zeros(small_ref.shape, F32)
    ns = sums_in.shape[0]
    small_ref[0:ns, :] = jnp.sum(sums_in[...], axis=1)
    small_ref[ns : ns + 49, :] = jnp.sum(acc_ref[...], axis=1)


def back_kernel(
    nbr_ref, cnt_ref, hw_ref, he_ref, gi_ref, ge_ref, dyt_ref, oi_ref, oe_ref, k_ref,
    out_ref, gx_ref,
    west_ref, east_ref, center_ref, full_ref, k8_ref,
):
    live = cnt_ref[0]
    spread_taps(k_ref, k8_ref, True)

    def place(r, carry):
        for h in range(2):
            g = full_width(gi_ref, ge_ref, h, r)
            o = full_width(oi_ref, oe_ref, h, r)
            for c in range(16):
                center_ref[h, 3 + r, c * 8 : c * 8 + 8, :] = g[c]
                full_ref[h, r, c * 8 : c * 8 + 8, :] = o[c]
        for t in range(8):
            for h in range(2):
                v = full_ref[h, r, pl.ds(t, 16, stride=8), :]
                out_ref[t, r, :, lanes(h)] = jnp.where(t < live, v, 0.0).astype(BF16)
        return carry

    lax.fori_loop(0, 16, place, 0)
    rims_of(center_ref, nbr_ref)
    side_rim(west_ref, hw_ref, nbr_ref, 2, 4, 6)
    side_rim(east_ref, he_ref, nbr_ref, 3, 5, 7)
    pads = (west_ref, center_ref, east_ref)

    def row(r, carry):
        for h in range(2):
            accs = conv_wide(pads, k8_ref, h, r, 0, 16)
            for c in range(16):
                cs = slice(c * 8, c * 8 + 8)
                full_ref[h, r, cs, :] = accs[c] + dyt_ref[h, r, cs, :]
        for t in range(8):
            for h in range(2):
                v = full_ref[h, r, pl.ds(t, 16, stride=8), :]
                gx_ref[t, r, :, lanes(h)] = jnp.where(t < live, v, 0.0).astype(BF16)
        return carry

    lax.fori_loop(0, 16, row, 0)


def shifted(block, axis, distance):
    n = lax.axis_size(axis)
    return lax.ppermute(block, axis, [((i - distance) % n, i) for i in range(n)])


def crossed(v, mask):
    n = lax.axis_size(AXES)
    return lax.ppermute(v, AXES, [(i, i ^ mask) for i in range(n)])


def stages():
    total = lax.axis_size(AXES)
    found, bit = [(1, 2)], 2
    while bit < total:
        size = min(4, total // bit)
        found.append((bit, size))
        bit *= size
    return found


def reduce_all(v):
    me = lax.axis_index(AXES)
    rows, width = v.shape
    for bit, size in stages():
        mine = (me // bit) % size
        parts = v.reshape(size, v.shape[0] // size, width)
        acc = lax.dynamic_index_in_dim(parts, mine, 0, keepdims=False).astype(F32)
        for k in range(1, size):
            sent = lax.dynamic_index_in_dim(parts, mine ^ k, 0, keepdims=False)
            acc = acc + crossed(sent, k * bit).astype(F32)
        v = acc.astype(BF16)
    for bit, size in stages()[::-1]:
        mine = (me // bit) % size
        out = jnp.zeros((size,) + v.shape, BF16)
        out = lax.dynamic_update_index_in_dim(out, v, mine, 0)
        for k in range(1, size):
            out = lax.dynamic_update_index_in_dim(out, crossed(v, k * bit), mine ^ k, 0)
        v = out.reshape(size * v.shape[0], width)
    return v


def reduce_small(v):
    for bit, size in stages():
        acc = v
        for k in range(1, size):
            acc = acc + crossed(v, k * bit)
        v = acc
    return v


def on_device(
    activations, cotangent, tile_count, neighbours, conv_kernel, conv_bias, norm_gain, norm_bias,
    proj_in, bias_in, proj_out, bias_out, layer_scale,
):
    x = activations[0]
    dy = cotangent[0]
    slots, edge, _, channels = x.shape
    hidden = proj_in.shape[1]
    taps = conv_kernel.reshape(TAPS * TAPS, channels)
    row = lambda v: v.reshape(1, -1)
    weights = (
        proj_in, proj_out, row(bias_in), row(bias_out), row(layer_scale), row(norm_gain), row(norm_bias),
        row(conv_bias),
    )

    def columns(lo):
        return x[:, :, lo : lo + RIM].transpose(1, 2, 0, 3).reshape(edge * RIM * slots, channels)

    from_east = shifted(columns(0), "space", -1)
    from_west = shifted(columns(edge - RIM), "space", 1)
    ns = hidden // 256 + 5
    half = (2, edge, edge * slots, LANES)
    k8 = pltpu.VMEM((2, TAPS * TAPS, 8, LANES), F32)
    side = (2, edge + 2 * RIM, RIM * slots, LANES)
    tall = (2, edge + 2 * RIM, edge * slots, LANES)
    inner = (2, edge, (edge - 2 * RIM) * slots, LANES)
    edges = (2, edge, 2 * RIM * slots, LANES)
    halo = (edge * RIM * slots, channels)
    dw_shape = (2 * channels, hidden)

    center, dyt, out_i, g_i, dw, sums = call(
        inner_kernel,
        [(tall, F32), (half, F32), (inner, F32), (inner, F32), (dw_shape, F32), ((ns, 8, channels), F32)],
        (neighbours, tile_count, x, dy, taps) + weights,
        [k8, pltpu.VMEM((4 * 10 * slots, channels), F32)],
        smem=2,
    )
    west, east, out_e, g_e, send_l, send_r, dw, sums = call(
        edge_kernel,
        [(side, F32), (side, F32), (edges, F32), (edges, F32), (halo, BF16), (halo, BF16),
         (dw_shape, F32), ((ns, 8, channels), F32)],
        (neighbours, from_west, from_east, center, dyt, dw, sums, taps) + weights,
        [k8, pltpu.VMEM((8 * 6 * slots, channels), F32)],
        smem=1,
    )
    grad_from_east = shifted(send_l, "space", -1)
    grad_from_west = shifted(send_r, "space", 1)
    dw = reduce_all(dw.astype(BF16))
    (small,) = call(
        tap_kernel,
        [((64, channels), F32)],
        (center, west, east, g_i, g_e, sums),
        [pltpu.VMEM((TAPS * TAPS, 8, channels), F32)],
    )
    small = reduce_small(small)
    out_tiles, grad_tiles = call(
        back_kernel,
        [((slots, edge, edge, channels), BF16)] * 2,
        (neighbours, tile_count, grad_from_west, grad_from_east, g_i, g_e, dyt, out_i, out_e, taps),
        [pltpu.VMEM(side, F32), pltpu.VMEM(side, F32), pltpu.VMEM(tall, F32), pltpu.VMEM(half, F32), k8],
        smem=2,
    )
    factor = 1.0 / math.sqrt(lax.axis_size("dp") * lax.axis_size("space") * slots * edge * edge)
    small = small * factor
    dw = dw.astype(F32) * factor
    nk = hidden // 256
    return (
        out_tiles[None],
        grad_tiles[None],
        small[ns : ns + 49].reshape(TAPS, TAPS, channels),
        small[nk + 4],
        small[nk + 2],
        small[nk + 3],
        dw[:channels],
        small[:nk].reshape(-1),
        dw[channels:].T,
        small[nk],
        small[nk + 1],
    )


def solution(mesh):
    tiles = P("dp", "space", None, None, None)
    return jax.shard_map(
        on_device,
        mesh=mesh,
        in_specs=(tiles, tiles, P("space"), P("space", None)) + (P(),) * 9,
        out_specs=(tiles, tiles) + (P(),) * 9,
        check_vma=False,
    )
```

```python
import functools
import math

import jax
import jax.numpy as jnp
import numpy as np
from jax import lax
from jax.experimental import pallas as pl
from jax.experimental.pallas import tpu as pltpu
from jax.sharding import PartitionSpec as P

ROOT_TWO_PI = 0.7978845608
CUBIC_TERM = 0.044715
EPSILON = 1e-06

F32 = jnp.float32
BF16 = jnp.bfloat16
LANES = 128
TAPS = 7
RIM = 3
AXES = ("space", "dp")
VMEM_LIMIT = 32 * 1024 * 1024
KEEP = True


def vmem_spec():
    return pl.BlockSpec(memory_space=pltpu.VMEM)


def smem_spec():
    return pl.BlockSpec(memory_space=pltpu.SMEM)


def call(body, outs, ins, scratch=(), smem=0, alias=None, after=(), token=False):
    n_ins = len(ins)
    n_out = len(outs) + token
    outs = list(outs) + [((8, LANES), F32, KEEP)] * token

    def kernel(*refs):
        rest = list(refs[n_ins + len(after) :])
        if token:
            rest.pop(n_out - 1)[...] = jnp.zeros((8, LANES), F32)
        body(*refs[:n_ins], *rest)

    res = pl.pallas_call(
        kernel,
        out_shape=tuple(pltpu.VMEM(o[0], o[1]) if len(o) > 2 else jax.ShapeDtypeStruct(o[0], o[1]) for o in outs),
        in_specs=[smem_spec()] * smem + [vmem_spec()] * (n_ins - smem + len(after)),
        out_specs=tuple(vmem_spec() for _ in outs),
        scratch_shapes=list(scratch),
        input_output_aliases=alias or {},
        compiler_params=pltpu.CompilerParams(vmem_limit_bytes=VMEM_LIMIT),
    )(*[placed(v) for v in (*ins, *after)])
    return tuple(Kept(r) if len(o) > 2 else r for r, o in zip(res, outs))


def placed(v):
    if isinstance(v, Kept):
        return pltpu.with_memory_space_constraint(v.value, pltpu.VMEM)
    if isinstance(v, Far):
        return pltpu.with_memory_space_constraint(v.value, pltpu.HBM)
    return v


class Far:
    def __init__(self, value):
        self.value = value


class Kept:
    def __init__(self, value):
        self.value = value


def slot_pick(nbr_ref, which):
    slots = nbr_ref.shape[0]
    row = lax.broadcasted_iota(jnp.int32, (slots, LANES), 0)
    ids = jnp.full((slots, LANES), -1, jnp.int32)
    for t in range(slots):
        ids = jnp.where(row == t, nbr_ref[t, which], ids)
    present = ids >= 0
    return jnp.where(present, lax.rem(ids, slots), 0), present


def take(v, pick):
    ids, present = pick
    return jnp.where(present, jnp.take_along_axis(v, ids, axis=0, mode="promise_in_bounds"), 0.0)


def lanes(h):
    return slice(h * LANES, (h + 1) * LANES)


def pad_col(pads, h, r, c):
    west, center, east = pads
    if c < RIM:
        return west[h, r, c * 8 : c * 8 + 8, :]
    c -= RIM
    if c < 16:
        return center[h, r, c * 8 : c * 8 + 8, :]
    c -= 16
    return east[h, r, c * 8 : c * 8 + 8, :]


def spread_taps(k_ref, k8_ref, flip):
    for h in range(2):
        for tap in range(TAPS * TAPS):
            i, j = divmod(TAPS * TAPS - 1 - tap if flip else tap, TAPS)
            k8_ref[h, tap] = jnp.broadcast_to(k_ref[i, j : j + 1, lanes(h)], (8, LANES))


def conv_wide(pads, k8_ref, h, r, c0, n):
    accs = [None] * n
    for i in range(TAPS):
        xs = [pad_col(pads, h, r + i, c0 + c) for c in range(n + TAPS - 1)]
        for j in range(TAPS):
            kk = k8_ref[h, i * TAPS + j]
            for c in range(n):
                term = xs[c + j] * kk
                accs[c] = term if accs[c] is None else accs[c] + term
    return accs


def conv_tall(pads, k8_ref, h, r0, rows, c0, n):
    accs = [[None] * n for _ in range(rows)]
    for j in range(TAPS):
        ks = [k8_ref[h, i * TAPS + j] for i in range(TAPS)]
        for p in range(rows + TAPS - 1):
            xs = [pad_col(pads, h, r0 + p, c0 + j + c) for c in range(n)]
            for q in range(max(0, p - TAPS + 1), min(rows, p + 1)):
                for c in range(n):
                    term = xs[c] * ks[p - q]
                    accs[q][c] = term if accs[q][c] is None else accs[q][c] + term
    return accs


def gelu_pair(pre):
    sq = pre * pre
    t = jnp.tanh(pre * (ROOT_TWO_PI + (ROOT_TWO_PI * CUBIC_TERM) * sq))
    half = 0.5 + 0.5 * t
    act = pre * half
    slope = half + act * (1.0 - t) * (ROOT_TWO_PI + (3.0 * ROOT_TWO_PI * CUBIC_TERM) * sq)
    return act, slope


def fold(v):
    return jnp.sum(v.reshape(v.shape[0] // 8, 8, v.shape[1]), axis=0)


def dot(a, b):
    return jnp.dot(a, b, preferred_element_type=F32)


def dot_t(a, b):
    return lax.dot_general(a, b, (((1,), (1,)), ((), ())), preferred_element_type=F32)


def dense_block(conv, x, dy, params, add_dw, sums_ref):
    win, wout, bias_in, bias_out, scale, gain, shift, conv_bias = params
    hidden = win.shape[1]
    channels = win.shape[0]
    conv = conv + conv_bias[...]
    centred = conv - jnp.mean(conv, axis=1, keepdims=True)
    inv_std = lax.rsqrt(jnp.mean(centred * centred, axis=1, keepdims=True) + EPSILON)
    normed = centred * inv_std
    unit = (normed * gain[...] + shift[...]).astype(BF16)
    gb = (dy * scale[...]).astype(BF16)
    unit_t = unit.T
    gb_t = gb.T
    branch = jnp.zeros(conv.shape, F32)
    grad_unit = jnp.zeros(conv.shape, F32)
    for k in range(0, hidden, 256):
        ks = slice(k, k + 256)
        pre = dot(unit, win[:, ks]) + bias_in[:, ks]
        act, slope = gelu_pair(pre)
        act = act.astype(BF16)
        gp = (dot_t(gb, wout[ks, :]) * slope).astype(BF16)
        branch = branch + dot(act, wout[ks, :])
        grad_unit = grad_unit + dot_t(gp, win[:, ks])
        add_dw(0, k, dot(unit_t, gp))
        add_dw(1, k, dot(gb_t, act))
        sums_ref[k // 256] += fold(gp.astype(F32))
    branch = branch + bias_out[...]
    out = x + scale[...] * branch
    scaled = grad_unit * gain[...]
    grad_conv = inv_std * (
        scaled
        - jnp.mean(scaled, axis=1, keepdims=True)
        - normed * jnp.mean(scaled * normed, axis=1, keepdims=True)
    )
    grad_conv = grad_conv.astype(BF16).astype(F32)
    nk = hidden // 256
    sums_ref[nk] += fold(gb.astype(F32))
    sums_ref[nk + 1] += fold(dy * branch)
    sums_ref[nk + 2] += fold(grad_unit * normed)
    sums_ref[nk + 3] += fold(grad_unit)
    sums_ref[nk + 4] += fold(grad_conv)
    return out, grad_conv


def rows_of(ref, r0, nr, c0, n):
    blocks = []
    for q in range(nr):
        blocks.append(jnp.concatenate([ref[h, r0 + q, c0 * 8 : (c0 + n) * 8, :] for h in range(2)], axis=1))
    return jnp.concatenate(blocks, axis=0)


def rims_of(center_ref, nbr_ref):
    north = slot_pick(nbr_ref, 0)
    south = slot_pick(nbr_ref, 1)
    for h in range(2):
        for q in range(RIM):
            for c in range(16):
                cs = slice(c * 8, c * 8 + 8)
                center_ref[h, q, cs, :] = take(center_ref[h, 16 + q, cs, :], north)
                center_ref[h, 19 + q, cs, :] = take(center_ref[h, 3 + q, cs, :], south)


def side_rim(side_ref, halo_ref, nbr_ref, straight, up, down):
    mid, top, low = (slot_pick(nbr_ref, w) for w in (straight, up, down))
    for h in range(2):
        for pair in range(24):
            v = halo_ref[pair * 16 : pair * 16 + 16, lanes(h)].astype(F32)
            for s in range(2):
                r, c = divmod(pair * 2 + s, RIM)
                cs = slice(c * 8, c * 8 + 8)
                part = v[s * 8 : s * 8 + 8]
                side_ref[h, 3 + r, cs, :] = take(part, mid)
                if r >= 13:
                    side_ref[h, r - 13, cs, :] = take(part, top)
                if r < 3:
                    side_ref[h, 19 + r, cs, :] = take(part, low)


def inner_kernel(
    nbr_ref, cnt_ref, place_ref, x_ref, dy_ref, k_ref, win, wout, bias_in, bias_out, scale, gain, shift, conv_bias,
    center_ref, dyt_ref, out_ref, g_ref, dw_ref, sums_ref,
    k8_ref, conv_ref,
):
    live = cnt_ref[0]
    channels = win.shape[0]
    spread_taps(k_ref, k8_ref, False)
    dw_ref[...] = jnp.zeros(dw_ref.shape, F32)
    sums_ref[...] = jnp.zeros(sums_ref.shape, F32)

    def turn(r, carry):
        for t in range(8):
            for h in range(2):
                center_ref[h, 3 + r, pl.ds(t, 16, stride=8), :] = x_ref[t, r, :, lanes(h)].astype(F32)
                dyv = dy_ref[t, r, :, lanes(h)].astype(F32)
                dyt_ref[h, r, pl.ds(t, 16, stride=8), :] = jnp.where(t < live, dyv, 0.0)
        return carry

    lax.fori_loop(0, 16, turn, 0)
    rims_of(center_ref, nbr_ref)
    params = (win, wout, bias_in, bias_out, scale, gain, shift, conv_bias)
    nr, n, c0 = 4, 10, 3
    cols = slice(c0 * 8, (c0 + n) * 8)
    pads = (None, center_ref, None)

    def add_dw(which, k, v):
        dw_ref[which * channels : (which + 1) * channels, k : k + 256] += v

    def block(m, carry):
        r0 = m * nr

        def conv(q, carry):
            for h in range(2):
                accs = conv_wide(pads, k8_ref, h, r0 + q, c0, n)
                conv_ref[pl.ds(pl.multiple_of(q * n * 8, 8), n * 8), lanes(h)] = jnp.concatenate(accs, axis=0)
            return carry

        lax.fori_loop(0, nr, conv, 0)
        x = rows_of(center_ref, r0 + 3, nr, c0, n)
        dy = rows_of(dyt_ref, r0, nr, c0, n)
        out, g = dense_block(conv_ref[...], x, dy, params, add_dw, sums_ref)
        for q in range(nr):
            for h in range(2):
                out_ref[h, r0 + q, cols, :] = out[q * n * 8 : (q + 1) * n * 8, lanes(h)]
                g_ref[h, 3 + r0 + q, cols, :] = g[q * n * 8 : (q + 1) * n * 8, lanes(h)]
        return carry

    lax.fori_loop(0, 16 // nr, block, 0)


def edge_kernel(
    nbr_ref, core_ref, hw_ref, he_ref, center_ref, dyt_ref, dw_in, sums_in, out_in, g_in,
    k_ref, win, wout, bias_in, bias_out, scale, gain, shift, conv_bias,
    west_ref, east_ref, out_ref, g_ref, send_l, send_r, own_ref, sent_ref, sums_ref,
    k8_ref, conv_ref, dw_ref,
):
    core = core_ref[0]
    channels = win.shape[0]
    hidden = win.shape[1]
    spread_taps(k_ref, k8_ref, False)
    sums_ref[...] = sums_in[...]
    side_rim(west_ref, hw_ref, nbr_ref, 2, 4, 6)
    side_rim(east_ref, he_ref, nbr_ref, 3, 5, 7)
    params = (win, wout, bias_in, bias_out, scale, gain, shift, conv_bias)
    pads = (west_ref, center_ref, east_ref)
    nr = 8
    n_blocks = 16 // nr

    for m in range(n_blocks):
        r0 = m * nr
        src, last = (dw_in, m == n_blocks - 1) if m == 0 else (dw_ref, m == n_blocks - 1)

        def add_dw(which, k, v, src=src, last=last):
            at = slice(which * channels, (which + 1) * channels), slice(k, k + 256)
            v = src[at] + v
            if not last:
                dw_ref[at] = v
                return
            if which == 1:
                v = v.T
            v = v.astype(BF16)
            for side in range(2):
                row = k * 2 + side * 256 if which == 0 else side * hidden + k
                piece = v[:, lanes(side)]

                @pl.when(core == which)
                def _():
                    own_ref[row : row + 256, :] = piece

                @pl.when(core != which)
                def _():
                    sent_ref[row : row + 256, :] = piece

        for h in range(2):
            for side, c0 in enumerate((0, 13)):
                accs = conv_tall(pads, k8_ref, h, r0, nr, c0, RIM)
                for q in range(nr):
                    base = (q * 2 + side) * 24
                    conv_ref[base : base + 24, lanes(h)] = jnp.concatenate(accs[q], axis=0)
        xs, dys = [], []
        for q in range(nr):
            for c0 in (0, 13):
                xs.append(rows_of(center_ref, r0 + 3 + q, 1, c0, RIM))
                dys.append(rows_of(dyt_ref, r0 + q, 1, c0, RIM))
        x = jnp.concatenate(xs, axis=0)
        dy = jnp.concatenate(dys, axis=0)
        out, g = dense_block(conv_ref[...], x, dy, params, add_dw, sums_ref)
        for q in range(nr):
            for side, c0 in enumerate((0, 13)):
                part = slice((q * 2 + side) * 24, (q * 2 + side) * 24 + 24)
                cols = slice(c0 * 8, c0 * 8 + 24)
                for h in range(2):
                    out_ref[h, r0 + q, cols, :] = out[part, lanes(h)]
                    g_ref[h, 3 + r0 + q, cols, :] = g[part, lanes(h)]
        for q in range(0, nr, 2):
            for side, send in enumerate((send_l, send_r)):
                v = jnp.concatenate(
                    [g[(q + s) * 48 + side * 24 : (q + s) * 48 + side * 24 + 24] for s in range(2)], axis=0
                )
                send[(r0 + q) * 24 : (r0 + q) * 24 + 48, :] = v.astype(BF16)


def turn_out(out_ref, src_ref, live, r):
    for t in range(8):
        for h in range(2):
            v = src_ref[h, r, pl.ds(t, 16, stride=8), :]
            out_ref[t, r, :, lanes(h)] = jnp.where(t < live, v, 0.0).astype(BF16)


def tiles_kernel(nbr_ref, cnt_ref, full_ref, g_in, out_ref, g_ref):
    live = cnt_ref[0]
    rims_of(g_ref, nbr_ref)

    def row(r, carry):
        turn_out(out_ref, full_ref, live, r)
        return carry

    lax.fori_loop(0, 16, row, 0)


def tap_kernel(h, center_ref, west_ref, east_ref, g_ref, acc_ref):
    pads = (west_ref, center_ref, east_ref)

    def row_tap(i, carry):
        def row(r, accs):
            g = [g_ref[h, 3 + r, c * 8 : c * 8 + 8, :] for c in range(16)]
            xs = [pad_col(pads, h, r + i, c) for c in range(22)]
            new = []
            for j in range(TAPS):
                terms = [xs[c + j] * g[c] for c in range(16)]
                while len(terms) > 1:
                    terms = [a + b for a, b in zip(terms[::2], terms[1::2])]
                new.append(accs[j] + terms[0])
            return tuple(new)

        accs = lax.fori_loop(0, 16, row, tuple(jnp.zeros((8, LANES), F32) for _ in range(TAPS)))
        for j in range(TAPS):
            acc_ref[i * TAPS + j] = accs[j]
        return carry

    lax.fori_loop(0, TAPS, row_tap, 0)


def small_kernel(tap0, tap1, sums, small_ref):
    ns = sums.shape[0]
    small_ref[...] = jnp.zeros(small_ref.shape, F32)
    small_ref[0:ns, :] = jnp.sum(sums[...], axis=1)
    small_ref[ns : ns + 49, lanes(0)] = jnp.sum(tap0[...], axis=1)
    small_ref[ns : ns + 49, lanes(1)] = jnp.sum(tap1[...], axis=1)


def sides_kernel(nbr_ref, hw_ref, he_ref, west_ref, east_ref):
    side_rim(west_ref, hw_ref, nbr_ref, 2, 4, 6)
    side_rim(east_ref, he_ref, nbr_ref, 3, 5, 7)


def back_kernel(first, last, cnt_ref, west_ref, east_ref, g_ref, dyt_ref, k_ref, *refs):
    gx_ref, full_ref, k8_ref = refs[-3:]
    live = cnt_ref[0]
    spread_taps(k_ref, k8_ref, True)
    pads = (west_ref, g_ref, east_ref)

    def row(r, carry):
        for h in range(2):
            accs = conv_wide(pads, k8_ref, h, r, 0, 16)
            for c in range(16):
                cs = slice(c * 8, c * 8 + 8)
                full_ref[h, r, cs, :] = accs[c] + dyt_ref[h, r, cs, :]
        turn_out(gx_ref, full_ref, live, r)
        return carry

    lax.fori_loop(first, last, row, 0)


def scatter_kernel(level, size, mine_ref, *refs):
    n_out = size
    held, outs = refs[:-n_out], refs[-n_out:]
    total = held[0][...].astype(F32)
    for h in held[1:]:
        total = total + h[...].astype(F32)
    total = total.astype(BF16)
    rows = total.shape[0] // size
    if size == 1:
        outs[0][...] = total
        return
    mine = mine_ref[level]
    for p in range(size):
        piece = total[p * rows : (p + 1) * rows]
        for k in range(size):

            @pl.when((mine ^ k) == p)
            def _(k=k, piece=piece):
                outs[k][...] = piece


def gather_kernel(level, size, mine_ref, *refs):
    parts, out = refs[:-1], refs[-1]
    rows = parts[0].shape[0]
    mine = mine_ref[level]
    for k in range(size):
        out[pl.ds(pl.multiple_of((mine ^ k) * rows, 16), rows), :] = parts[k][...]


def last_kernel(factor, core_ref, own_ref, other_ref, win_ref, wout_ref):
    core = core_ref[0]
    hidden = wout_ref.shape[0]

    def put_in(ref):
        for b in range(hidden // LANES):
            win_ref[:, b * LANES : (b + 1) * LANES] = ref[b * 256 : b * 256 + 256, :].astype(F32) * factor

    def put_out(ref):
        for side in range(2):
            wout_ref[:, lanes(side)] = ref[side * hidden : (side + 1) * hidden, :].astype(F32) * factor

    @pl.when(core == 0)
    def _():
        put_in(own_ref)
        put_out(other_ref)

    @pl.when(core != 0)
    def _():
        put_in(other_ref)
        put_out(own_ref)


def shifted(block, axis, distance):
    n = lax.axis_size(axis)
    return lax.ppermute(block, axis, [((i - distance) % n, i) for i in range(n)])


def crossed(v, mask):
    n = lax.axis_size(AXES)
    return lax.ppermute(v, AXES, [(i, i ^ mask) for i in range(n)])


def groups():
    total = lax.axis_size(AXES)
    found, bit = [(1, 2)], 2
    while bit < total:
        size = min(4, total // bit)
        found.append((bit, size))
        bit *= size
    return found


def on_device(
    activations, cotangent, tile_count, neighbours, conv_kernel, conv_bias, norm_gain, norm_bias,
    proj_in, bias_in, proj_out, bias_out, layer_scale,
):
    x = activations[0]
    dy = cotangent[0]
    slots, edge, _, channels = x.shape
    hidden = proj_in.shape[1]
    row = lambda v: v.reshape(1, -1)
    weights = (
        proj_in, proj_out, row(bias_in), row(bias_out), row(layer_scale), row(norm_gain), row(norm_bias),
        row(conv_bias),
    )
    weights = tuple(Far(w) for w in weights)
    conv_kernel = Far(conv_kernel)
    places = np.array([[(d // bit) % size for bit, size in groups()] for d in range(lax.axis_size(AXES))], np.int32)
    place = lax.dynamic_index_in_dim(jnp.asarray(places), lax.axis_index(AXES), 0, keepdims=False)

    def columns(lo):
        return x[:, :, lo : lo + RIM].transpose(1, 2, 0, 3).reshape(edge * RIM * slots, channels)

    from_east = shifted(columns(0), "space", -1)
    from_west = shifted(columns(edge - RIM), "space", 1)
    ns = hidden // 256 + 5
    half = (2, edge, edge * slots, LANES)
    k8 = pltpu.VMEM((2, TAPS * TAPS, 8, LANES), F32)
    side = (2, edge + 2 * RIM, RIM * slots, LANES)
    tall = (2, edge + 2 * RIM, edge * slots, LANES)
    halo = (edge * RIM * slots, channels)
    dw_shape = (2 * channels, hidden)
    sums_shape = (ns, 8, channels)
    tiles = (slots, edge, edge, channels)
    travel = (channels * hidden // LANES, LANES)

    center, dyt, full, g, dw, sums = call(
        inner_kernel,
        [(tall, F32, KEEP), (half, F32, KEEP), (half, F32, KEEP), (tall, F32, KEEP), (dw_shape, F32, KEEP),
         (sums_shape, F32, KEEP)],
        (neighbours, tile_count, place, Far(x), Far(dy), conv_kernel) + weights,
        [k8, pltpu.VMEM((4 * 10 * slots, channels), F32)],
        smem=3,
    )
    west, east, full, g, send_l, send_r, held, sent, sums = call(
        edge_kernel,
        [(side, F32, KEEP), (side, F32, KEEP), (half, F32, KEEP), (tall, F32, KEEP), (halo, BF16), (halo, BF16),
         (travel, BF16), (travel, BF16), (sums_shape, F32, KEEP)],
        (neighbours, place, from_west, from_east, center, dyt, dw, sums, full, g, conv_kernel) + weights,
        [k8, pltpu.VMEM((8 * 6 * slots, channels), F32), pltpu.VMEM(dw_shape, F32)],
        smem=2,
        alias={8: 2, 9: 3},
    )
    later = groups()[1:]
    arrived = [crossed(sent, 1)]
    grad_from_east = shifted(send_l, "space", -1)
    grad_from_west = shifted(send_r, "space", 1)

    out_tiles, g, done = call(
        tiles_kernel, [(tiles, BF16), (tall, F32, KEEP)], (neighbours, tile_count, full, g), smem=2, alias={3: 1},
        token=True,
    )
    filler = (done,)
    taps = []

    def tap(h):
        v, done = call(
            functools.partial(tap_kernel, h), [((TAPS * TAPS, 8, LANES), F32, KEEP)], (center, west, east, g),
            after=(begun,), token=True,
        )
        taps.append(v)
        return done

    for n, (bit, size) in enumerate(later):
        level = n + 1
        held, *parts, begun = call(
            functools.partial(scatter_kernel, level, size),
            [((held.shape[0] // size, LANES), BF16)] * size,
            (place, held, *arrived),
            smem=1,
            after=filler,
            token=True,
        )
        arrived = [crossed(p, k * bit) for k, p in enumerate(parts, 1)]
        filler = (tap(n),) if n < 2 else ()
    small, done = call(small_kernel, [((64, channels), F32)], (*taps, sums), after=filler, token=True)
    held, begun = call(
        functools.partial(scatter_kernel, 0, 1), [(held.shape, BF16)], (place, held, *arrived), smem=1, after=(done,),
        token=True,
    )

    sides = None
    gx = None
    for n, (bit, size) in enumerate(later[::-1]):
        level = len(later) - n
        parts = [held] + [crossed(held, k * bit) for k in range(1, size)]
        small = sum((crossed(small, k * bit) for k in range(1, size)), small)
        filler = ()
        if n < 2:
            if n == 0:
                sides = call(
                    sides_kernel, [(side, F32, KEEP)] * 2, (neighbours, grad_from_west, grad_from_east), smem=1,
                    after=(begun,),
                )
            gx, done = call(
                functools.partial(back_kernel, n * edge // 2, (n + 1) * edge // 2),
                [(tiles, BF16, KEEP)],
                (tile_count, *sides, g, dyt, conv_kernel) + ((gx,) if n else ()),
                [pltpu.VMEM(half, F32), k8],
                smem=1,
                alias={6: 0} if n else None,
                after=(begun,),
                token=True,
            )
            filler = (done,)
        held, begun = call(
            functools.partial(gather_kernel, level, size), [((held.shape[0] * size, LANES), BF16)],
            (place, *parts), smem=1, after=filler, token=True,
        )
    small = small + crossed(small, 1)
    factor = 1.0 / math.sqrt(lax.axis_size("dp") * lax.axis_size("space") * slots * edge * edge)
    grad_in, grad_out = call(
        functools.partial(last_kernel, factor),
        [((channels, hidden), F32), ((hidden, channels), F32)],
        (place, held, crossed(held, 1)),
        smem=1,
    )
    small = small * factor
    nk = hidden // 256
    return (
        out_tiles[None],
        gx.value[None],
        small[ns : ns + 49].reshape(TAPS, TAPS, channels),
        small[nk + 4],
        small[nk + 2],
        small[nk + 3],
        grad_in,
        small[:nk].reshape(-1),
        grad_out,
        small[nk],
        small[nk + 1],
    )


def solution(mesh):
    tiles = P("dp", "space", None, None, None)
    return jax.shard_map(
        on_device,
        mesh=mesh,
        in_specs=(tiles, tiles, P("space"), P("space", None)) + (P(),) * 9,
        out_specs=(tiles, tiles) + (P(),) * 9,
        check_vma=False,
    )
```

```python
import functools
import math

import jax
import jax.numpy as jnp
from jax import lax
from jax.experimental import pallas as pl
from jax.experimental.pallas import tpu as pltpu
from jax.sharding import PartitionSpec as P

ROOT_TWO_PI = 0.7978845608
CUBIC_TERM = 0.044715
EPSILON = 1e-06

F32 = jnp.float32
BF16 = jnp.bfloat16
LANES = 128
TAPS = 7
RIM = 3
AXES = ("space", "dp")
VMEM_LIMIT = 32 * 1024 * 1024
KEEP = True


def vmem_spec():
    return pl.BlockSpec(memory_space=pltpu.VMEM)


def smem_spec():
    return pl.BlockSpec(memory_space=pltpu.SMEM)


def call(body, outs, ins, scratch=(), smem=0, alias=None, after=(), token=False):
    n_ins = len(ins)
    n_out = len(outs) + token
    outs = list(outs) + [((8, LANES), F32, KEEP)] * token

    def kernel(*refs):
        rest = list(refs[n_ins + len(after) :])
        if token:
            rest.pop(n_out - 1)[...] = jnp.zeros((8, LANES), F32)
        body(*refs[:n_ins], *rest)

    res = pl.pallas_call(
        kernel,
        out_shape=tuple(pltpu.VMEM(o[0], o[1]) if len(o) > 2 else jax.ShapeDtypeStruct(o[0], o[1]) for o in outs),
        in_specs=[smem_spec()] * smem + [vmem_spec()] * (n_ins - smem + len(after)),
        out_specs=tuple(vmem_spec() for _ in outs),
        scratch_shapes=list(scratch),
        input_output_aliases=alias or {},
        compiler_params=pltpu.CompilerParams(vmem_limit_bytes=VMEM_LIMIT),
    )(*[placed(v) for v in (*ins, *after)])
    return tuple(Kept(r) if len(o) > 2 else r for r, o in zip(res, outs))


def placed(v):
    if isinstance(v, Kept):
        return pltpu.with_memory_space_constraint(v.value, pltpu.VMEM)
    if isinstance(v, Far):
        return pltpu.with_memory_space_constraint(v.value, pltpu.HBM)
    return v


class Far:
    def __init__(self, value):
        self.value = value


class Kept:
    def __init__(self, value):
        self.value = value


def slot_pick(nbr_ref, which):
    slots = nbr_ref.shape[0]
    row = lax.broadcasted_iota(jnp.int32, (slots, LANES), 0)
    ids = jnp.full((slots, LANES), -1, jnp.int32)
    for t in range(slots):
        ids = jnp.where(row == t, nbr_ref[t, which], ids)
    present = ids >= 0
    return jnp.where(present, lax.rem(ids, slots), 0), present


def take(v, pick):
    ids, present = pick
    return jnp.where(present, jnp.take_along_axis(v, ids, axis=0, mode="promise_in_bounds"), 0.0)


def lanes(h):
    return slice(h * LANES, (h + 1) * LANES)


def pad_col(pads, h, r, c):
    west, center, east = pads
    if c < RIM:
        return west[h, r, c * 8 : c * 8 + 8, :]
    c -= RIM
    if c < 16:
        return center[h, r, c * 8 : c * 8 + 8, :]
    c -= 16
    return east[h, r, c * 8 : c * 8 + 8, :]


def spread_taps(k_ref, k8_ref, flip):
    for h in range(2):
        for tap in range(TAPS * TAPS):
            i, j = divmod(TAPS * TAPS - 1 - tap if flip else tap, TAPS)
            k8_ref[h, tap] = jnp.broadcast_to(k_ref[i, j : j + 1, lanes(h)], (8, LANES))


def conv_wide(pads, k8_ref, h, r, c0, n):
    accs = [None] * n
    for i in range(TAPS):
        xs = [pad_col(pads, h, r + i, c0 + c) for c in range(n + TAPS - 1)]
        for j in range(TAPS):
            kk = k8_ref[h, i * TAPS + j]
            for c in range(n):
                term = xs[c + j] * kk
                accs[c] = term if accs[c] is None else accs[c] + term
    return accs


def conv_tall(pads, k8_ref, h, r0, rows, c0, n):
    accs = [[None] * n for _ in range(rows)]
    for j in range(TAPS):
        ks = [k8_ref[h, i * TAPS + j] for i in range(TAPS)]
        for p in range(rows + TAPS - 1):
            xs = [pad_col(pads, h, r0 + p, c0 + j + c) for c in range(n)]
            for q in range(max(0, p - TAPS + 1), min(rows, p + 1)):
                for c in range(n):
                    term = xs[c] * ks[p - q]
                    accs[q][c] = term if accs[q][c] is None else accs[q][c] + term
    return accs


def gelu_pair(pre):
    sq = pre * pre
    t = jnp.tanh(pre * (ROOT_TWO_PI + (ROOT_TWO_PI * CUBIC_TERM) * sq))
    half = 0.5 + 0.5 * t
    act = pre * half
    slope = half + act * (1.0 - t) * (ROOT_TWO_PI + (3.0 * ROOT_TWO_PI * CUBIC_TERM) * sq)
    return act, slope


def fold(v):
    return jnp.sum(v.reshape(v.shape[0] // 8, 8, v.shape[1]), axis=0)


def dot(a, b):
    return jnp.dot(a, b, preferred_element_type=F32)


def dot_t(a, b):
    return lax.dot_general(a, b, (((1,), (1,)), ((), ())), preferred_element_type=F32)


def dense_block(conv, x, dy, params, add_dw, add_sum):
    win, wout, bias_in, bias_out, scale, gain, shift, conv_bias = params
    hidden = win.shape[1]
    channels = win.shape[0]
    conv = conv + conv_bias[...]
    centred = conv - jnp.mean(conv, axis=1, keepdims=True)
    inv_std = lax.rsqrt(jnp.mean(centred * centred, axis=1, keepdims=True) + EPSILON)
    normed = centred * inv_std
    unit = (normed * gain[...] + shift[...]).astype(BF16)
    gb = (dy * scale[...]).astype(BF16)
    unit_t = unit.T
    gb_t = gb.T
    branch = jnp.zeros(conv.shape, F32)
    grad_unit = jnp.zeros(conv.shape, F32)
    for k in range(0, hidden, 256):
        ks = slice(k, k + 256)
        pre = dot(unit, win[:, ks]) + bias_in[:, ks]
        act, slope = gelu_pair(pre)
        act = act.astype(BF16)
        gp = (dot_t(gb, wout[ks, :]) * slope).astype(BF16)
        branch = branch + dot(act, wout[ks, :])
        grad_unit = grad_unit + dot_t(gp, win[:, ks])
        add_dw(0, k, dot(unit_t, gp))
        add_dw(1, k, dot(gb_t, act))
        add_sum(k // 256, fold(gp.astype(F32)))
    branch = branch + bias_out[...]
    out = x + scale[...] * branch
    scaled = grad_unit * gain[...]
    grad_conv = inv_std * (
        scaled
        - jnp.mean(scaled, axis=1, keepdims=True)
        - normed * jnp.mean(scaled * normed, axis=1, keepdims=True)
    )
    grad_conv = grad_conv.astype(BF16).astype(F32)
    nk = hidden // 256
    add_sum(nk + 0, fold(gb.astype(F32)))
    add_sum(nk + 1, fold(dy * branch))
    add_sum(nk + 2, fold(grad_unit * normed))
    add_sum(nk + 3, fold(grad_unit))
    add_sum(nk + 4, fold(grad_conv))
    return out, grad_conv


def rows_of(ref, r0, nr, c0, n):
    blocks = []
    for q in range(nr):
        blocks.append(jnp.concatenate([ref[h, r0 + q, c0 * 8 : (c0 + n) * 8, :] for h in range(2)], axis=1))
    return jnp.concatenate(blocks, axis=0)


def rims_of(center_ref, nbr_ref):
    north = slot_pick(nbr_ref, 0)
    south = slot_pick(nbr_ref, 1)
    for h in range(2):
        for q in range(RIM):
            for c in range(16):
                cs = slice(c * 8, c * 8 + 8)
                center_ref[h, q, cs, :] = take(center_ref[h, 16 + q, cs, :], north)
                center_ref[h, 19 + q, cs, :] = take(center_ref[h, 3 + q, cs, :], south)


def side_rim(side_ref, halo_ref, nbr_ref, straight, up, down):
    mid, top, low = (slot_pick(nbr_ref, w) for w in (straight, up, down))
    for h in range(2):
        for pair in range(24):
            v = halo_ref[pair * 16 : pair * 16 + 16, lanes(h)].astype(F32)
            for s in range(2):
                r, c = divmod(pair * 2 + s, RIM)
                cs = slice(c * 8, c * 8 + 8)
                part = v[s * 8 : s * 8 + 8]
                side_ref[h, 3 + r, cs, :] = take(part, mid)
                if r >= 13:
                    side_ref[h, r - 13, cs, :] = take(part, top)
                if r < 3:
                    side_ref[h, 19 + r, cs, :] = take(part, low)


def inner_kernel(
    n_place, nbr_ref, cnt_ref, *refs,
):
    (x_ref, dy_ref, k_ref, win, wout, bias_in, bias_out, scale, gain, shift, conv_bias) = refs[n_place : n_place + 11]
    center_ref, dyt_ref, out_ref, g_ref, dw_ref, sums_ref, k8_ref, win_kept, wout_kept, vec_kept, conv_ref = refs[
        n_place + 11 :
    ]
    live = cnt_ref[0]
    channels = win.shape[0]
    spread_taps(k_ref, k8_ref, False)
    win_kept[...] = win[...]
    wout_kept[...] = wout[...]
    for i, v in enumerate((bias_in, bias_out, scale, gain, shift, conv_bias)):
        vec_kept[i : i + 1, 0 : v.shape[1]] = v[...]

    def turn(r, carry):
        for t in range(8):
            for h in range(2):
                center_ref[h, 3 + r, pl.ds(t, 16, stride=8), :] = x_ref[t, r, :, lanes(h)].astype(F32)
                dyv = dy_ref[t, r, :, lanes(h)].astype(F32)
                dyt_ref[h, r, pl.ds(t, 16, stride=8), :] = jnp.where(t < live, dyv, 0.0)
        return carry

    lax.fori_loop(0, 16, turn, 0)
    rims_of(center_ref, nbr_ref)
    params = (win, wout, bias_in, bias_out, scale, gain, shift, conv_bias)
    n, c0 = 10, 3
    cols = slice(c0 * 8, (c0 + n) * 8)
    pads = (None, center_ref, None)

    def add_dw(which, k, v):
        dw_ref[which * channels : (which + 1) * channels, k : k + 256] = v

    def add_sum(which, v):
        sums_ref[which] = v

    def conv(q, carry):
        for h in range(2):
            accs = conv_wide(pads, k8_ref, h, q, c0, n)
            conv_ref[pl.ds(pl.multiple_of(q * n * 8, 8), n * 8), lanes(h)] = jnp.concatenate(accs, axis=0)
        return carry

    lax.fori_loop(0, 16, conv, 0)
    x = rows_of(center_ref, 3, 16, c0, n)
    dy = rows_of(dyt_ref, 0, 16, c0, n)
    out, g = dense_block(conv_ref[...], x, dy, params, add_dw, add_sum)
    for q in range(16):
        for h in range(2):
            out_ref[h, q, cols, :] = out[q * n * 8 : (q + 1) * n * 8, lanes(h)]
            g_ref[h, 3 + q, cols, :] = g[q * n * 8 : (q + 1) * n * 8, lanes(h)]


def edge_kernel(
    nbr_ref, place_ref, hw_ref, he_ref, center_ref, dyt_ref, dw_in, sums_in, out_in, g_in, k8_ref, win, wout, vec,
    west_ref, east_ref, out_ref, g_ref, send_l, send_r, own_ref, sent_ref, sums_ref,
    conv_ref, travel_ref,
):
    core = place_ref[0]
    channels, hidden = win.shape
    side_rim(west_ref, hw_ref, nbr_ref, 2, 4, 6)
    side_rim(east_ref, he_ref, nbr_ref, 3, 5, 7)
    widths = (hidden,) + (channels,) * 5
    params = (win, wout) + tuple(vec.at[i : i + 1, 0:w] for i, w in enumerate(widths))
    pads = (west_ref, center_ref, east_ref)

    def add_dw(which, k, v):
        v = dw_in[which * channels : (which + 1) * channels, k : k + 256] + v
        if which == 1:
            v = v.T
        v = v.astype(BF16)
        for side in range(2):
            row = k * 2 + side * 256 if which == 0 else side * hidden + k
            travel_ref[which, row : row + 256, :] = v[:, lanes(side)]

    def add_sum(which, v):
        sums_ref[which] = sums_in[which] + v

    def conv(m, carry):
        r0 = m * 8
        for h in range(2):
            for side, c0 in enumerate((0, 13)):
                accs = conv_tall(pads, k8_ref, h, r0, 8, c0, RIM)
                for q in range(8):
                    at = pl.multiple_of(((r0 + q) * 2 + side) * 24, 8)
                    conv_ref[pl.ds(at, 24), lanes(h)] = jnp.concatenate(accs[q], axis=0)
        return carry

    lax.fori_loop(0, 2, conv, 0)
    xs, dys = [], []
    for q in range(16):
        for c0 in (0, 13):
            xs.append(rows_of(center_ref, 3 + q, 1, c0, RIM))
            dys.append(rows_of(dyt_ref, q, 1, c0, RIM))
    x = jnp.concatenate(xs, axis=0)
    dy = jnp.concatenate(dys, axis=0)
    out, g = dense_block(conv_ref[...], x, dy, params, add_dw, add_sum)
    for q in range(16):
        for side, c0 in enumerate((0, 13)):
            part = slice((q * 2 + side) * 24, (q * 2 + side) * 24 + 24)
            cols = slice(c0 * 8, c0 * 8 + 24)
            for h in range(2):
                out_ref[h, q, cols, :] = out[part, lanes(h)]
                g_ref[h, 3 + q, cols, :] = g[part, lanes(h)]
    for q in range(0, 16, 2):
        for side, send in enumerate((send_l, send_r)):
            v = [g[(q + s) * 48 + side * 24 : (q + s) * 48 + side * 24 + 24] for s in range(2)]
            send[q * 24 : q * 24 + 48, :] = jnp.concatenate(v, axis=0).astype(BF16)
    own_ref[...] = travel_ref[core]
    sent_ref[...] = travel_ref[1 - core]


def turn_out(out_ref, src_ref, live, r):
    for t in range(8):
        for h in range(2):
            v = src_ref[h, r, pl.ds(t, 16, stride=8), :]
            out_ref[t, r, :, lanes(h)] = jnp.where(t < live, v, 0.0).astype(BF16)


def tiles_kernel(cnt_ref, full_ref, out_ref):
    live = cnt_ref[0]

    def row(r, carry):
        turn_out(out_ref, full_ref, live, r)
        return carry

    lax.fori_loop(0, 16, row, 0)


def tap_kernel(h, center_ref, west_ref, east_ref, g_ref, acc_ref):
    pads = (west_ref, center_ref, east_ref)

    def row_tap(i, carry):
        def row(r, accs):
            g = [g_ref[h, 3 + r, c * 8 : c * 8 + 8, :] for c in range(16)]
            xs = [pad_col(pads, h, r + i, c) for c in range(22)]
            new = []
            for j in range(TAPS):
                terms = [xs[c + j] * g[c] for c in range(16)]
                while len(terms) > 1:
                    terms = [a + b for a, b in zip(terms[::2], terms[1::2])]
                new.append(accs[j] + terms[0])
            return tuple(new)

        accs = lax.fori_loop(0, 16, row, tuple(jnp.zeros((8, LANES), F32) for _ in range(TAPS)))
        for j in range(TAPS):
            acc_ref[i * TAPS + j] = accs[j]
        return carry

    lax.fori_loop(0, TAPS, row_tap, 0)


def sides_kernel(nbr_ref, hw_ref, he_ref, g_in, west_ref, east_ref, g_ref):
    rims_of(g_ref, nbr_ref)
    side_rim(west_ref, hw_ref, nbr_ref, 2, 4, 6)
    side_rim(east_ref, he_ref, nbr_ref, 3, 5, 7)


def back_kernel(first, last, cnt_ref, west_ref, east_ref, g_ref, dyt_ref, k_ref, *refs):
    gx_ref, full_ref, k8_ref = refs[-3:]
    live = cnt_ref[0]
    spread_taps(k_ref, k8_ref, True)
    pads = (west_ref, g_ref, east_ref)
    if len(refs) > 3:
        gx_ref[:, :first] = refs[0][...]

    def row(r, carry):
        for h in range(2):
            accs = conv_wide(pads, k8_ref, h, r, 0, 16)
            for c in range(16):
                cs = slice(c * 8, c * 8 + 8)
                full_ref[h, r, cs, :] = accs[c] + dyt_ref[h, r, cs, :]
        turn_out(gx_ref, full_ref, live, r)
        return carry

    lax.fori_loop(first, last, row, 0)


def added(held):
    total = held[0][...].astype(F32)
    for h in held[1:]:
        total = total + h[...].astype(F32)
    return total.astype(BF16)


def scatter_kernel(size, place_ref, *refs):
    held, outs = refs[:-size], refs[-size:]
    total = added(held)
    rows = total.shape[0] // size
    mine = place_ref[0]
    for p in range(size):
        piece = total[p * rows : (p + 1) * rows]
        for k in range(size):

            @pl.when((mine ^ k) == p)
            def _(k=k, piece=piece):
                outs[k][...] = piece


def finish_kernel(tap0, tap1, sums, *refs):
    held, out = refs[:-1], refs[-1]
    ns = sums.shape[0]
    total = added(held)
    rows = total.shape[0]
    out[0:rows, :] = total
    dense = jnp.sum(sums[...], axis=1)
    rest = jnp.zeros((64 - ns - 49, LANES), F32)
    for h, tap in enumerate((tap0, tap1)):
        part = jnp.concatenate([dense[:, lanes(h)], jnp.sum(tap[...], axis=1), rest], axis=0)
        out[rows + 64 * h : rows + 64 * h + 64, :] = part.astype(BF16)


def gather_kernel(place_ref, *refs):
    parts, out = refs[:-1], refs[-1]
    rows = parts[0].shape[0] - LANES
    mine = place_ref[0]
    total = jnp.zeros((LANES, LANES), F32)
    for k, part in enumerate(parts):
        out[pl.ds(pl.multiple_of((mine ^ k) * rows, 16), rows), :] = part[0:rows, :]
        total = total + part[rows : rows + LANES, :].astype(F32)
    out[len(parts) * rows : len(parts) * rows + LANES, :] = total.astype(BF16)


def last_kernel(
    factor, place_ref, own_ref, other_ref,
    taps_ref, conv_bias_ref, gain_ref, shift_ref, win_ref, bias_in_ref, wout_ref, bias_out_ref, scale_ref,
):
    core = place_ref[0]
    hidden = wout_ref.shape[0]
    rows = 2 * hidden

    def put_in(ref):
        for b in range(hidden // LANES):
            win_ref[:, b * LANES : (b + 1) * LANES] = ref[b * 256 : b * 256 + 256, :].astype(F32) * factor

    def put_out(ref):
        for side in range(2):
            wout_ref[:, lanes(side)] = ref[side * hidden : (side + 1) * hidden, :].astype(F32) * factor

    @pl.when(core == 0)
    def _():
        put_in(own_ref)
        put_out(other_ref)

    @pl.when(core != 0)
    def _():
        put_in(other_ref)
        put_out(own_ref)

    nk = hidden // 256
    for h in range(2):
        at = slice(rows + 64 * h, rows + 64 * h + 64)
        small = (own_ref[at, :].astype(F32) + other_ref[at, :].astype(F32)) * factor
        for k in range(nk):
            bias_in_ref[:, k * 256 + h * LANES : k * 256 + (h + 1) * LANES] = small[k : k + 1]
        for k, ref in enumerate((bias_out_ref, scale_ref, gain_ref, shift_ref, conv_bias_ref)):
            ref[:, lanes(h)] = small[nk + k : nk + k + 1]
        for i in range(TAPS):
            at = nk + 5 + i * TAPS
            taps_ref[i, :, lanes(h)] = small[at : at + TAPS]


def shifted(block, axis, distance):
    n = lax.axis_size(axis)
    return lax.ppermute(block, axis, [((i - distance) % n, i) for i in range(n)])


def crossed(v, mask):
    n = lax.axis_size(AXES)
    return lax.ppermute(v, AXES, [(i, i ^ mask) for i in range(n)])


def groups():
    total = lax.axis_size(AXES)
    found, bit = [(1, 2)], 2
    while bit < total:
        size = min(4, total // bit)
        found.append((bit, size))
        bit *= size
    return found


def on_device(
    activations, cotangent, tile_count, neighbours, conv_kernel, conv_bias, norm_gain, norm_bias,
    proj_in, bias_in, proj_out, bias_out, layer_scale,
):
    x = activations[0]
    dy = cotangent[0]
    slots, edge, _, channels = x.shape
    hidden = proj_in.shape[1]
    row = lambda v: v.reshape(1, -1)
    weights = (
        proj_in, proj_out, row(bias_in), row(bias_out), row(layer_scale), row(norm_gain), row(norm_bias),
        row(conv_bias),
    )
    weights = tuple(Far(w) for w in weights)
    conv_kernel = Far(conv_kernel)
    me = lax.axis_index(AXES)
    place = [((me // bit) % size).astype(jnp.int32).reshape(1) for bit, size in groups()]
    neighbours = Far(neighbours)

    def columns(lo):
        return x[:, :, lo : lo + RIM].transpose(1, 2, 0, 3).reshape(edge * RIM * slots, channels)

    from_east = shifted(columns(0), "space", -1)
    from_west = shifted(columns(edge - RIM), "space", 1)
    ns = hidden // 256 + 5
    half = (2, edge, edge * slots, LANES)
    k8 = pltpu.VMEM((2, TAPS * TAPS, 8, LANES), F32)
    side = (2, edge + 2 * RIM, RIM * slots, LANES)
    tall = (2, edge + 2 * RIM, edge * slots, LANES)
    halo = (edge * RIM * slots, channels)
    dw_shape = (2 * channels, hidden)
    sums_shape = (ns, 8, channels)
    tiles = (slots, edge, edge, channels)
    travel = (channels * hidden // LANES, LANES)

    spread = (2, TAPS * TAPS, 8, LANES)
    center, dyt, full, g, dw, sums, *kept = call(
        functools.partial(inner_kernel, len(place)),
        [(tall, F32, KEEP), (half, F32, KEEP), (half, F32, KEEP), (tall, F32, KEEP), (dw_shape, F32, KEEP),
         (sums_shape, F32, KEEP), (spread, F32, KEEP), (proj_in.shape, BF16, KEEP), (proj_out.shape, BF16, KEEP),
         ((8, hidden), F32, KEEP)],
        (neighbours, tile_count, *place, Far(x), Far(dy), conv_kernel) + weights,
        [pltpu.VMEM((edge * (edge - 2 * RIM) * slots, channels), F32)],
        smem=2 + len(place),
    )
    west, east, full, g, send_l, send_r, held, sent, sums = call(
        edge_kernel,
        [(side, F32, KEEP), (side, F32, KEEP), (half, F32, KEEP), (tall, F32, KEEP), (halo, BF16), (halo, BF16),
         (travel, BF16), (travel, BF16), (sums_shape, F32, KEEP)],
        (neighbours, place[0], from_west, from_east, center, dyt, dw, sums, full, g, *kept),
        [pltpu.VMEM((edge * 2 * RIM * slots, channels), F32), pltpu.VMEM((2,) + travel, BF16)],
        smem=2,
        alias={8: 2, 9: 3},
    )
    later = groups()[1:]
    arrived = [crossed(sent, 1)]
    grad_from_east = shifted(send_l, "space", -1)
    grad_from_west = shifted(send_r, "space", 1)

    filler = ()
    taps = []

    def tap(h):
        v, done = call(
            functools.partial(tap_kernel, h), [((TAPS * TAPS, 8, LANES), F32, KEEP)], (center, west, east, g),
            after=(begun,), token=True,
        )
        taps.append(v)
        return done

    sides = None
    gx = ()
    cuts = [0, 4, 9, edge]

    def back():
        nonlocal gx
        first = gx[0].value.shape[1] if gx else 0
        last = cuts[cuts.index(first) + 1]
        *gx, done = call(
            functools.partial(back_kernel, first, last),
            [((slots, last, edge, channels), BF16, KEEP) if last < edge else (tiles, BF16)],
            (tile_count, *sides, g, dyt, conv_kernel, *gx),
            [pltpu.VMEM(half, F32), k8],
            smem=1,
            after=(begun,),
            token=True,
        )
        return done

    for n, (bit, size) in enumerate(later):
        held, *parts, begun = call(
            functools.partial(scatter_kernel, size),
            [((held.shape[0] // size, LANES), BF16)] * size,
            (place[n + 1], held, *arrived),
            smem=1,
            after=filler,
            token=True,
        )
        arrived = [crossed(p, k * bit) for k, p in enumerate(parts, 1)]
        filler = ()
        if n == 0:
            filler = (tap(0), tap(1))
        if n == 1:
            *sides, g = call(
                sides_kernel, [(side, F32, KEEP), (side, F32, KEEP), (tall, F32, KEEP)],
                (neighbours, grad_from_west, grad_from_east, g), smem=1, alias={3: 2}, after=(begun,),
            )
            filler = (back(),)
    held, begun = call(
        finish_kernel, [((held.shape[0] + LANES, LANES), BF16)], (*taps, sums, held, *arrived), after=filler, token=True
    )

    for n, (bit, size) in enumerate(later[::-1]):
        parts = [held] + [crossed(held, k * bit) for k in range(1, size)]
        filler = (back(),) if n < 2 else ()
        rows = (held.shape[0] - LANES) * size + LANES
        held, begun = call(
            gather_kernel, [((rows, LANES), BF16)],
            (place[len(later) - n], *parts), smem=1, after=filler, token=True,
        )
    out_tiles, done = call(tiles_kernel, [(tiles, BF16)], (tile_count, full), smem=1, after=(begun,), token=True)
    factor = 1.0 / math.sqrt(lax.axis_size("dp") * lax.axis_size("space") * slots * edge * edge)
    vec = ((1, channels), F32)
    small = [((TAPS, TAPS, channels), F32), vec, vec, vec]
    grads = call(
        functools.partial(last_kernel, factor),
        [*small, ((channels, hidden), F32), ((1, hidden), F32), ((hidden, channels), F32), vec, vec],
        (place[0], held, crossed(held, 1)),
        smem=1,
        after=(done,),
    )
    grads = [v.reshape(-1) if v.shape[0] == 1 else v for v in grads]
    return (out_tiles[None], gx[0][None], *grads)


def solution(mesh):
    tiles = P("dp", "space", None, None, None)
    return jax.shard_map(
        on_device,
        mesh=mesh,
        in_specs=(tiles, tiles, P("space"), P("space", None)) + (P(),) * 9,
        out_specs=(tiles, tiles) + (P(),) * 9,
        check_vma=False,
    )
```

```python
import functools
import math

import jax
import jax.numpy as jnp
from jax import lax
from jax.experimental import pallas as pl
from jax.experimental.pallas import tpu as pltpu
from jax.sharding import PartitionSpec as P

ROOT_TWO_PI = 0.7978845608
CUBIC_TERM = 0.044715
EPSILON = 1e-06

F32 = jnp.float32
BF16 = jnp.bfloat16
LANES = 128
TAPS = 7
RIM = 3
AXES = ("space", "dp")
VMEM_LIMIT = 32 * 1024 * 1024
KEEP = True
WORK = 8_000_000_000


def vmem_spec():
    return pl.BlockSpec(memory_space=pltpu.VMEM)


def smem_spec():
    return pl.BlockSpec(memory_space=pltpu.SMEM)


def call(body, outs, ins, scratch=(), smem=0, alias=None, after=(), token=False, work=0):
    n_ins = len(ins)
    n_out = len(outs) + token
    outs = list(outs) + [((8, LANES), F32, KEEP)] * token

    def kernel(*refs):
        rest = list(refs[n_ins + len(after) :])
        if token:
            rest.pop(n_out - 1)[...] = jnp.zeros((8, LANES), F32)
        body(*refs[:n_ins], *rest)

    res = pl.pallas_call(
        kernel,
        out_shape=tuple(pltpu.VMEM(o[0], o[1]) if len(o) > 2 else jax.ShapeDtypeStruct(o[0], o[1]) for o in outs),
        in_specs=[smem_spec()] * smem + [vmem_spec()] * (n_ins - smem + len(after)),
        out_specs=tuple(vmem_spec() for _ in outs),
        scratch_shapes=list(scratch),
        input_output_aliases=alias or {},
        cost_estimate=pl.CostEstimate(flops=work, transcendentals=0, bytes_accessed=work // 256) if work else None,
        compiler_params=pltpu.CompilerParams(vmem_limit_bytes=VMEM_LIMIT),
    )(*[placed(v) for v in (*ins, *after)])
    return tuple(Kept(r) if len(o) > 2 else r for r, o in zip(res, outs))


def placed(v):
    if isinstance(v, Kept):
        return pltpu.with_memory_space_constraint(v.value, pltpu.VMEM)
    if isinstance(v, Far):
        return pltpu.with_memory_space_constraint(v.value, pltpu.HBM)
    return v


class Far:
    def __init__(self, value):
        self.value = value


class Kept:
    def __init__(self, value):
        self.value = value


def slot_pick(nbr_ref, which):
    slots = nbr_ref.shape[0]
    row = lax.broadcasted_iota(jnp.int32, (slots, LANES), 0)
    ids = jnp.full((slots, LANES), -1, jnp.int32)
    for t in range(slots):
        ids = jnp.where(row == t, nbr_ref[t, which], ids)
    present = ids >= 0
    return jnp.where(present, lax.rem(ids, slots), 0), present


def take(v, pick):
    ids, present = pick
    return jnp.where(present, jnp.take_along_axis(v, ids, axis=0, mode="promise_in_bounds"), 0.0)


def lanes(h):
    return slice(h * LANES, (h + 1) * LANES)


def pad_col(pads, h, r, c):
    west, center, east = pads
    if c < RIM:
        return west[h, r, c * 8 : c * 8 + 8, :]
    c -= RIM
    if c < 16:
        return center[h, r, c * 8 : c * 8 + 8, :]
    c -= 16
    return east[h, r, c * 8 : c * 8 + 8, :]


def spread_taps(k_ref, k8_ref, flip):
    for h in range(2):
        for tap in range(TAPS * TAPS):
            i, j = divmod(TAPS * TAPS - 1 - tap if flip else tap, TAPS)
            k8_ref[h, tap] = jnp.broadcast_to(k_ref[i, j : j + 1, lanes(h)], (8, LANES))


def conv_wide(pads, k8_ref, h, r, c0, n):
    accs = [None] * n
    for i in range(TAPS):
        xs = [pad_col(pads, h, r + i, c0 + c) for c in range(n + TAPS - 1)]
        for j in range(TAPS):
            kk = k8_ref[h, i * TAPS + j]
            for c in range(n):
                term = xs[c + j] * kk
                accs[c] = term if accs[c] is None else accs[c] + term
    return accs


def conv_tall(pads, k8_ref, h, r0, rows, c0, n):
    accs = [[None] * n for _ in range(rows)]
    for j in range(TAPS):
        ks = [k8_ref[h, i * TAPS + j] for i in range(TAPS)]
        for p in range(rows + TAPS - 1):
            xs = [pad_col(pads, h, r0 + p, c0 + j + c) for c in range(n)]
            for q in range(max(0, p - TAPS + 1), min(rows, p + 1)):
                for c in range(n):
                    term = xs[c] * ks[p - q]
                    accs[q][c] = term if accs[q][c] is None else accs[q][c] + term
    return accs


def gelu_pair(pre):
    sq = pre * pre
    t = jnp.tanh(pre * (ROOT_TWO_PI + (ROOT_TWO_PI * CUBIC_TERM) * sq))
    half = 0.5 + 0.5 * t
    act = pre * half
    slope = half + act * (1.0 - t) * (ROOT_TWO_PI + (3.0 * ROOT_TWO_PI * CUBIC_TERM) * sq)
    return act, slope


def fold(v):
    return jnp.sum(v.reshape(v.shape[0] // 8, 8, v.shape[1]), axis=0)


def dot(a, b):
    return jnp.dot(a, b, preferred_element_type=F32)


def dot_t(a, b):
    return lax.dot_general(a, b, (((1,), (1,)), ((), ())), preferred_element_type=F32)


def dense_block(conv, x, dy, params, add_dw, add_sum):
    win, wout, bias_in, bias_out, scale, gain, shift, conv_bias = params
    hidden = win.shape[1]
    channels = win.shape[0]
    conv = conv + conv_bias[...]
    centred = conv - jnp.mean(conv, axis=1, keepdims=True)
    inv_std = lax.rsqrt(jnp.mean(centred * centred, axis=1, keepdims=True) + EPSILON)
    normed = centred * inv_std
    unit = (normed * gain[...] + shift[...]).astype(BF16)
    gb = (dy * scale[...]).astype(BF16)
    unit_t = unit.T
    gb_t = gb.T
    acts, gps = [], []
    for k in range(0, hidden, 256):
        ks = slice(k, k + 256)
        act, slope = gelu_pair(dot(unit, win[:, ks]) + bias_in[:, ks])
        gp = (dot_t(gb, wout[ks, :]) * slope).astype(BF16)
        add_sum(k // 256, fold(gp.astype(F32)))
        acts.append(act.astype(BF16))
        gps.append(gp)
    for k, act, gp in zip(range(0, hidden, 256), acts, gps):
        add_dw(0, k, dot(unit_t, gp))
        add_dw(1, k, dot(gb_t, act))
    branch = dot(jnp.concatenate(acts, axis=1), wout[...])
    grad_unit = dot_t(jnp.concatenate(gps, axis=1), win[...])
    branch = branch + bias_out[...]
    out = x + scale[...] * branch
    scaled = grad_unit * gain[...]
    grad_conv = inv_std * (
        scaled
        - jnp.mean(scaled, axis=1, keepdims=True)
        - normed * jnp.mean(scaled * normed, axis=1, keepdims=True)
    )
    grad_conv = grad_conv.astype(BF16).astype(F32)
    nk = hidden // 256
    add_sum(nk + 0, fold(gb.astype(F32)))
    add_sum(nk + 1, fold(dy * branch))
    add_sum(nk + 2, fold(grad_unit * normed))
    add_sum(nk + 3, fold(grad_unit))
    add_sum(nk + 4, fold(grad_conv))
    return out, grad_conv


def rows_of(ref, r0, nr, c0, n):
    blocks = []
    for q in range(nr):
        blocks.append(jnp.concatenate([ref[h, r0 + q, c0 * 8 : (c0 + n) * 8, :] for h in range(2)], axis=1))
    return jnp.concatenate(blocks, axis=0)


def rims_of(center_ref, nbr_ref):
    north = slot_pick(nbr_ref, 0)
    south = slot_pick(nbr_ref, 1)
    for h in range(2):
        for q in range(RIM):
            for c in range(16):
                cs = slice(c * 8, c * 8 + 8)
                center_ref[h, q, cs, :] = take(center_ref[h, 16 + q, cs, :], north)
                center_ref[h, 19 + q, cs, :] = take(center_ref[h, 3 + q, cs, :], south)


def side_rim(side_ref, halo_ref, nbr_ref, straight, up, down):
    mid, top, low = (slot_pick(nbr_ref, w) for w in (straight, up, down))
    for h in range(2):
        for pair in range(24):
            v = halo_ref[pair * 16 : pair * 16 + 16, lanes(h)].astype(F32)
            for s in range(2):
                r, c = divmod(pair * 2 + s, RIM)
                cs = slice(c * 8, c * 8 + 8)
                part = v[s * 8 : s * 8 + 8]
                side_ref[h, 3 + r, cs, :] = take(part, mid)
                if r >= 13:
                    side_ref[h, r - 13, cs, :] = take(part, top)
                if r < 3:
                    side_ref[h, 19 + r, cs, :] = take(part, low)


def inner_kernel(
    n_place, nbr_ref, cnt_ref, *refs,
):
    (x_ref, dy_ref, k_ref, win, wout, bias_in, bias_out, scale, gain, shift, conv_bias) = refs[n_place : n_place + 11]
    center_ref, dyt_ref, conv_ref, k8_ref, win_kept, wout_kept, vec_kept = refs[n_place + 11 :]
    live = cnt_ref[0]
    spread_taps(k_ref, k8_ref, False)
    win_kept[...] = win[...]
    wout_kept[...] = wout[...]
    for i, v in enumerate((bias_in, bias_out, scale, gain, shift, conv_bias)):
        vec_kept[i : i + 1, 0 : v.shape[1]] = v[...]

    def turn(r, carry):
        for t in range(8):
            for h in range(2):
                center_ref[h, 3 + r, pl.ds(t, 16, stride=8), :] = x_ref[t, r, :, lanes(h)].astype(F32)
                dyv = dy_ref[t, r, :, lanes(h)].astype(F32)
                dyt_ref[h, r, pl.ds(t, 16, stride=8), :] = jnp.where(t < live, dyv, 0.0)
        return carry

    lax.fori_loop(0, 16, turn, 0)
    rims_of(center_ref, nbr_ref)
    n, c0 = 10, 3
    pads = (None, center_ref, None)

    def conv(q, carry):
        for h in range(2):
            accs = conv_wide(pads, k8_ref, h, q, c0, n)
            conv_ref[h, q, c0 * 8 : (c0 + n) * 8, :] = jnp.concatenate(accs, axis=0)
        return carry

    lax.fori_loop(0, 16, conv, 0, unroll=2)


def edge_kernel(
    nbr_ref, hw_ref, he_ref, center_ref, dyt_ref, k8_ref, win, wout, vec,
    west_ref, east_ref, out_ref, g_ref, send_l, send_r, dw_ref, sums_ref,
    conv_ref,
):
    channels = win.shape[0]
    side_rim(west_ref, hw_ref, nbr_ref, 2, 4, 6)
    side_rim(east_ref, he_ref, nbr_ref, 3, 5, 7)
    params = (win, wout) + vectors(vec, win)
    pads = (west_ref, center_ref, east_ref)

    def add_dw(which, k, v):
        dw_ref[which * channels : (which + 1) * channels, k : k + 256] = v

    def add_sum(which, v):
        sums_ref[which] = v

    def conv(m, carry):
        r0 = m * 8
        for h in range(2):
            for side, c0 in enumerate((0, 13)):
                accs = conv_tall(pads, k8_ref, h, r0, 8, c0, RIM)
                for q in range(8):
                    at = pl.multiple_of(((r0 + q) * 2 + side) * 24, 8)
                    conv_ref[pl.ds(at, 24), lanes(h)] = jnp.concatenate(accs[q], axis=0)
        return carry

    lax.fori_loop(0, 2, conv, 0)
    xs, dys = [], []
    for q in range(16):
        for c0 in (0, 13):
            xs.append(rows_of(center_ref, 3 + q, 1, c0, RIM))
            dys.append(rows_of(dyt_ref, q, 1, c0, RIM))
    x = jnp.concatenate(xs, axis=0)
    dy = jnp.concatenate(dys, axis=0)
    out, g = dense_block(conv_ref[...], x, dy, params, add_dw, add_sum)
    for q in range(16):
        for side, c0 in enumerate((0, 13)):
            part = slice((q * 2 + side) * 24, (q * 2 + side) * 24 + 24)
            cols = slice(c0 * 8, c0 * 8 + 24)
            for h in range(2):
                out_ref[h, q, cols, :] = out[part, lanes(h)]
                g_ref[h, 3 + q, cols, :] = g[part, lanes(h)]
    for q in range(0, 16, 2):
        for side, send in enumerate((send_l, send_r)):
            v = [g[(q + s) * 48 + side * 24 : (q + s) * 48 + side * 24 + 24] for s in range(2)]
            send[q * 24 : q * 24 + 48, :] = jnp.concatenate(v, axis=0).astype(BF16)


def vectors(vec, win):
    channels, hidden = win.shape
    return tuple(vec.at[i : i + 1, 0:w] for i, w in enumerate((hidden,) + (channels,) * 5))


def middle_kernel(
    place_ref, center_ref, dyt_ref, conv_ref, dw_in, sums_in, out_in, g_in, win, wout, vec,
    out_ref, g_ref, own_ref, sent_ref, sums_ref,
    travel_ref,
):
    core = place_ref[0]
    channels, hidden = win.shape
    params = (win, wout) + vectors(vec, win)
    n, c0 = 10, 3
    cols = slice(c0 * 8, (c0 + n) * 8)

    def add_dw(which, k, v):
        v = dw_in[which * channels : (which + 1) * channels, k : k + 256] + v
        if which == 1:
            v = v.T
        v = v.astype(BF16)
        for side in range(2):
            row = k * 2 + side * 256 if which == 0 else side * hidden + k
            travel_ref[which, row : row + 256, :] = v[:, lanes(side)]

    def add_sum(which, v):
        sums_ref[which] = sums_in[which] + v

    x = rows_of(center_ref, 3, 16, c0, n)
    dy = rows_of(dyt_ref, 0, 16, c0, n)
    out, g = dense_block(rows_of(conv_ref, 0, 16, c0, n), x, dy, params, add_dw, add_sum)
    for q in range(16):
        for h in range(2):
            out_ref[h, q, cols, :] = out[q * n * 8 : (q + 1) * n * 8, lanes(h)]
            g_ref[h, 3 + q, cols, :] = g[q * n * 8 : (q + 1) * n * 8, lanes(h)]
    own_ref[...] = travel_ref[core]
    sent_ref[...] = travel_ref[1 - core]


def turn_out(out_ref, src_ref, live, r):
    for t in range(8):
        for h in range(2):
            v = src_ref[h, r, pl.ds(t, 16, stride=8), :]
            out_ref[t, r, :, lanes(h)] = jnp.where(t < live, v, 0.0).astype(BF16)


def tiles_kernel(cnt_ref, full_ref, out_ref):
    live = cnt_ref[0]

    def row(r, carry):
        turn_out(out_ref, full_ref, live, r)
        return carry

    lax.fori_loop(0, 16, row, 0)


def tap_kernel(h, center_ref, west_ref, east_ref, g_ref, acc_ref):
    pads = (west_ref, center_ref, east_ref)

    def row_tap(i, carry):
        def row(r, accs):
            g = [g_ref[h, 3 + r, c * 8 : c * 8 + 8, :] for c in range(16)]
            xs = [pad_col(pads, h, r + i, c) for c in range(22)]
            new = []
            for j in range(TAPS):
                terms = [xs[c + j] * g[c] for c in range(16)]
                while len(terms) > 1:
                    terms = [a + b for a, b in zip(terms[::2], terms[1::2])]
                new.append(accs[j] + terms[0])
            return tuple(new)

        accs = lax.fori_loop(0, 16, row, tuple(jnp.zeros((8, LANES), F32) for _ in range(TAPS)), unroll=4)
        for j in range(TAPS):
            acc_ref[i * TAPS + j] = accs[j]
        return carry

    lax.fori_loop(0, TAPS, row_tap, 0)


def sides_kernel(nbr_ref, hw_ref, he_ref, g_in, west_ref, east_ref, g_ref):
    rims_of(g_ref, nbr_ref)
    side_rim(west_ref, hw_ref, nbr_ref, 2, 4, 6)
    side_rim(east_ref, he_ref, nbr_ref, 3, 5, 7)


def back_kernel(first, last, cnt_ref, west_ref, east_ref, g_ref, dyt_ref, k_ref, *refs):
    gx_ref, full_ref, k8_ref = refs[-3:]
    live = cnt_ref[0]
    spread_taps(k_ref, k8_ref, True)
    pads = (west_ref, g_ref, east_ref)
    if len(refs) > 3:
        gx_ref[:, :first] = refs[0][...]

    def row(r, carry):
        for h in range(2):
            accs = conv_wide(pads, k8_ref, h, r, 0, 16)
            for c in range(16):
                cs = slice(c * 8, c * 8 + 8)
                full_ref[h, r, cs, :] = accs[c] + dyt_ref[h, r, cs, :]
        turn_out(gx_ref, full_ref, live, r)
        return carry

    lax.fori_loop(first, last, row, 0)


def added(held):
    total = held[0][...].astype(F32)
    for h in held[1:]:
        total = total + h[...].astype(F32)
    return total.astype(BF16)


def scatter_kernel(size, place_ref, *refs):
    held, outs = refs[:-size], refs[-size:]
    total = added(held)
    rows = total.shape[0] // size
    mine = place_ref[0]
    for p in range(size):
        piece = total[p * rows : (p + 1) * rows]
        for k in range(size):

            @pl.when((mine ^ k) == p)
            def _(k=k, piece=piece):
                outs[k][...] = piece


def finish_kernel(tap0, tap1, sums, *refs):
    held, out = refs[:-1], refs[-1]
    ns = sums.shape[0]
    total = added(held)
    rows = total.shape[0]
    out[0:rows, :] = total
    dense = jnp.sum(sums[...], axis=1)
    rest = jnp.zeros((64 - ns - 49, LANES), F32)
    for h, tap in enumerate((tap0, tap1)):
        part = jnp.concatenate([dense[:, lanes(h)], jnp.sum(tap[...], axis=1), rest], axis=0)
        out[rows + 64 * h : rows + 64 * h + 64, :] = part.astype(BF16)


def gather_kernel(place_ref, *refs):
    parts, out = refs[:-1], refs[-1]
    rows = parts[0].shape[0] - LANES
    mine = place_ref[0]
    total = jnp.zeros((LANES, LANES), F32)
    for k, part in enumerate(parts):
        at = mine ^ k
        out[pl.ds(pl.multiple_of(at * rows, 16), rows), :] = part[0:rows, :]
        total = total + part[rows : rows + LANES, :].astype(F32)
    out[len(parts) * rows : len(parts) * rows + LANES, :] = total.astype(BF16)


def last_kernel(
    factor, place_ref, own_ref, other_ref,
    taps_ref, conv_bias_ref, gain_ref, shift_ref, win_ref, bias_in_ref, wout_ref, bias_out_ref, scale_ref,
):
    core = place_ref[0]
    hidden = wout_ref.shape[0]
    rows = 2 * hidden

    def put_in(ref):
        for b in range(hidden // LANES):
            win_ref[:, b * LANES : (b + 1) * LANES] = ref[b * 256 : b * 256 + 256, :].astype(F32) * factor

    def put_out(ref):
        for side in range(2):
            wout_ref[:, lanes(side)] = ref[side * hidden : (side + 1) * hidden, :].astype(F32) * factor

    @pl.when(core == 0)
    def _():
        put_in(own_ref)
        put_out(other_ref)

    @pl.when(core != 0)
    def _():
        put_in(other_ref)
        put_out(own_ref)

    nk = hidden // 256
    for h in range(2):
        at = slice(rows + 64 * h, rows + 64 * h + 64)
        small = (own_ref[at, :].astype(F32) + other_ref[at, :].astype(F32)) * factor
        for k in range(nk):
            bias_in_ref[:, k * 256 + h * LANES : k * 256 + (h + 1) * LANES] = small[k : k + 1]
        for k, ref in enumerate((bias_out_ref, scale_ref, gain_ref, shift_ref, conv_bias_ref)):
            ref[:, lanes(h)] = small[nk + k : nk + k + 1]
        for i in range(TAPS):
            at = nk + 5 + i * TAPS
            taps_ref[i, :, lanes(h)] = small[at : at + TAPS]


def shifted(block, axis, distance):
    n = lax.axis_size(axis)
    return lax.ppermute(block, axis, [((i - distance) % n, i) for i in range(n)])


def crossed(v, mask):
    n = lax.axis_size(AXES)
    return lax.ppermute(v, AXES, [(i, i ^ mask) for i in range(n)])


def groups():
    total = lax.axis_size(AXES)
    found, bit = [(1, 2)], 2
    while bit < total:
        size = min(4, total // bit)
        found.append((bit, size))
        bit *= size
    return found


def on_device(
    activations, cotangent, tile_count, neighbours, conv_kernel, conv_bias, norm_gain, norm_bias,
    proj_in, bias_in, proj_out, bias_out, layer_scale,
):
    x = activations[0]
    dy = cotangent[0]
    slots, edge, _, channels = x.shape
    hidden = proj_in.shape[1]
    row = lambda v: v.reshape(1, -1)
    weights = (
        proj_in, proj_out, row(bias_in), row(bias_out), row(layer_scale), row(norm_gain), row(norm_bias),
        row(conv_bias),
    )
    weights = tuple(Far(w) for w in weights)
    conv_kernel = Far(conv_kernel)
    me = lax.axis_index(AXES)
    place = {g: ((me // g[0]) % g[1]).astype(jnp.int32).reshape(1) for g in groups()}
    neighbours = Far(neighbours)

    def columns(lo):
        return x[:, :, lo : lo + RIM].transpose(1, 2, 0, 3).reshape(edge * RIM * slots, channels)

    from_east = shifted(columns(0), "space", -1)
    from_west = shifted(columns(edge - RIM), "space", 1)
    ns = hidden // 256 + 5
    half = (2, edge, edge * slots, LANES)
    k8 = pltpu.VMEM((2, TAPS * TAPS, 8, LANES), F32)
    side = (2, edge + 2 * RIM, RIM * slots, LANES)
    tall = (2, edge + 2 * RIM, edge * slots, LANES)
    halo = (edge * RIM * slots, channels)
    sums_shape = (ns, 8, channels)
    tiles = (slots, edge, edge, channels)
    travel = (channels * hidden // LANES, LANES)
    dw_shape = (2 * channels, hidden)

    spread = (2, TAPS * TAPS, 8, LANES)
    center, dyt, conv, *kept = call(
        functools.partial(inner_kernel, len(place)),
        [(tall, F32, KEEP), (half, F32, KEEP), (half, F32, KEEP), (spread, F32, KEEP), (proj_in.shape, BF16, KEEP),
         (proj_out.shape, BF16, KEEP), ((8, hidden), F32, KEEP)],
        (neighbours, tile_count, *place.values(), Far(x), Far(dy), conv_kernel) + weights,
        smem=2 + len(place),
    )
    west, east, full, g, send_l, send_r, dw, sums = call(
        edge_kernel,
        [(side, F32, KEEP), (side, F32, KEEP), (half, F32, KEEP), (tall, F32, KEEP), (halo, BF16), (halo, BF16),
         (dw_shape, F32, KEEP), (sums_shape, F32, KEEP)],
        (neighbours, from_west, from_east, center, dyt, *kept),
        [pltpu.VMEM((edge * 2 * RIM * slots, channels), F32)],
        smem=1,
    )
    grad_from_east = shifted(send_l, "space", -1)
    grad_from_west = shifted(send_r, "space", 1)
    full, g, held, sent, sums = call(
        middle_kernel,
        [(half, F32, KEEP), (tall, F32, KEEP), (travel, BF16), (travel, BF16), (sums_shape, F32, KEEP)],
        (place[1, 2], center, dyt, conv, dw, sums, full, g, *kept[1:]),
        [pltpu.VMEM((2,) + travel, BF16)],
        smem=1,
        alias={6: 0, 7: 1},
    )
    later = groups()[1:]
    arrived = [crossed(sent, 1)]

    *sides, g, done = call(
        sides_kernel, [(side, F32, KEEP), (side, F32, KEEP), (tall, F32, KEEP)],
        (neighbours, grad_from_west, grad_from_east, g), smem=1, alias={3: 2}, token=True, work=WORK,
    )
    filler = (done,)
    taps = []

    def tap(h):
        v, done = call(
            functools.partial(tap_kernel, h), [((TAPS * TAPS, 8, LANES), F32, KEEP)], (center, west, east, g),
            after=(begun,), token=True, work=WORK,
        )
        taps.append(v)
        return done


    gx = ()
    cuts = [0, 6, 10, edge]

    def back():
        nonlocal gx
        first = gx[0].value.shape[1] if gx else 0
        last = cuts[cuts.index(first) + 1]
        *gx, done = call(
            functools.partial(back_kernel, first, last),
            [((slots, last, edge, channels), BF16, KEEP) if last < edge else (tiles, BF16)],
            (tile_count, *sides, g, dyt, conv_kernel, *gx),
            [pltpu.VMEM(half, F32), k8],
            smem=1,
            after=(begun,),
            token=True,
        )
        return done

    for n, (bit, size) in enumerate(later):
        held, *parts, begun = call(
            functools.partial(scatter_kernel, size),
            [((held.shape[0] // size, LANES), BF16)] * size,
            (place[bit, size], held, *arrived),
            smem=1,
            after=filler,
            token=True,
        )
        arrived = [crossed(p, k * bit) for k, p in enumerate(parts, 1)]
        filler = ()
        if n == 0:
            filler = (tap(0), tap(1))
        if n == 1:
            filler = (back(),)
    held, begun = call(
        finish_kernel, [((held.shape[0] + LANES, LANES), BF16)], (*taps, sums, held, *arrived), after=filler, token=True
    )

    for n, (bit, size) in enumerate(later[::-1]):
        parts = [held] + [crossed(held, k * bit) for k in range(1, size)]
        filler = (back(),) if n < 2 else ()
        rows = (held.shape[0] - LANES) * size + LANES
        held, begun = call(
            gather_kernel, [((rows, LANES), BF16)],
            (place[bit, size], *parts), smem=1, after=filler, token=True,
        )
    out_tiles, done = call(tiles_kernel, [(tiles, BF16)], (tile_count, full), smem=1, after=(begun,), token=True)
    factor = 1.0 / math.sqrt(lax.axis_size("dp") * lax.axis_size("space") * slots * edge * edge)
    vec = ((1, channels), F32)
    small = [((TAPS, TAPS, channels), F32), vec, vec, vec]
    grads = call(
        functools.partial(last_kernel, factor),
        [*small, ((channels, hidden), F32), ((1, hidden), F32), ((hidden, channels), F32), vec, vec],
        (place[1, 2], held, crossed(held, 1)),
        smem=1,
        after=(done,),
    )
    grads = [v.reshape(-1) if v.shape[0] == 1 else v for v in grads]
    return (out_tiles[None], gx[0][None], *grads)


def solution(mesh):
    tiles = P("dp", "space", None, None, None)
    return jax.shard_map(
        on_device,
        mesh=mesh,
        in_specs=(tiles, tiles, P("space"), P("space", None)) + (P(),) * 9,
        out_specs=(tiles, tiles) + (P(),) * 9,
        check_vma=False,
    )
```

```python
import functools
import math

import jax
import jax.numpy as jnp
from jax import lax
from jax.experimental import pallas as pl
from jax.experimental.pallas import tpu as pltpu
from jax.sharding import PartitionSpec as P

ROOT_TWO_PI = 0.7978845608
CUBIC_TERM = 0.044715
EPSILON = 1e-06

F32 = jnp.float32
BF16 = jnp.bfloat16
LANES = 128
TAPS = 7
RIM = 3
AXES = ("space", "dp")
VMEM_LIMIT = 32 * 1024 * 1024
KEEP = True
WORK = 8_000_000_000


def vmem_spec():
    return pl.BlockSpec(memory_space=pltpu.VMEM)


def smem_spec():
    return pl.BlockSpec(memory_space=pltpu.SMEM)


def call(body, outs, ins, scratch=(), smem=0, alias=None, after=(), token=False, work=0):
    n_ins = len(ins)
    n_out = len(outs) + token
    outs = list(outs) + [((8, LANES), F32, KEEP)] * token

    def kernel(*refs):
        rest = list(refs[n_ins + len(after) :])
        if token:
            rest.pop(n_out - 1)[...] = jnp.zeros((8, LANES), F32)
        body(*refs[:n_ins], *rest)

    res = pl.pallas_call(
        kernel,
        out_shape=tuple(pltpu.VMEM(o[0], o[1]) if len(o) > 2 else jax.ShapeDtypeStruct(o[0], o[1]) for o in outs),
        in_specs=[smem_spec()] * smem + [vmem_spec()] * (n_ins - smem + len(after)),
        out_specs=tuple(vmem_spec() for _ in outs),
        scratch_shapes=list(scratch),
        input_output_aliases=alias or {},
        cost_estimate=pl.CostEstimate(flops=work, transcendentals=0, bytes_accessed=work // 256) if work else None,
        compiler_params=pltpu.CompilerParams(vmem_limit_bytes=VMEM_LIMIT),
    )(*[placed(v) for v in (*ins, *after)])
    return tuple(Kept(r) if len(o) > 2 else r for r, o in zip(res, outs))


def placed(v):
    if isinstance(v, Kept):
        return pltpu.with_memory_space_constraint(v.value, pltpu.VMEM)
    if isinstance(v, Far):
        return pltpu.with_memory_space_constraint(v.value, pltpu.HBM)
    return v


class Far:
    def __init__(self, value):
        self.value = value


class Kept:
    def __init__(self, value):
        self.value = value


def slot_pick(nbr_ref, which):
    slots = nbr_ref.shape[0]
    row = lax.broadcasted_iota(jnp.int32, (slots, LANES), 0)
    ids = jnp.full((slots, LANES), -1, jnp.int32)
    for t in range(slots):
        ids = jnp.where(row == t, nbr_ref[t, which], ids)
    present = ids >= 0
    return jnp.where(present, lax.rem(ids, slots), 0), present


def take(v, pick):
    ids, present = pick
    return jnp.where(present, jnp.take_along_axis(v, ids, axis=0, mode="promise_in_bounds"), 0.0)


def lanes(h):
    return slice(h * LANES, (h + 1) * LANES)


def pad_col(pads, h, r, c):
    west, center, east = pads
    if c < RIM:
        return west[h, r, c * 8 : c * 8 + 8, :]
    c -= RIM
    if c < 16:
        return center[h, r, c * 8 : c * 8 + 8, :]
    c -= 16
    return east[h, r, c * 8 : c * 8 + 8, :]


def spread_taps(k_ref, k8_ref, flip):
    for h in range(2):
        for tap in range(TAPS * TAPS):
            i, j = divmod(TAPS * TAPS - 1 - tap if flip else tap, TAPS)
            k8_ref[h, tap] = jnp.broadcast_to(k_ref[i, j : j + 1, lanes(h)], (8, LANES))


def conv_wide(pads, k8_ref, h, r, c0, n):
    accs = [None] * n
    for i in range(TAPS):
        xs = [pad_col(pads, h, r + i, c0 + c) for c in range(n + TAPS - 1)]
        for j in range(TAPS):
            kk = k8_ref[h, i * TAPS + j]
            for c in range(n):
                term = xs[c + j] * kk
                accs[c] = term if accs[c] is None else accs[c] + term
    return accs


def conv_tall(pads, k8_ref, h, r0, rows, c0, n):
    accs = [[None] * n for _ in range(rows)]
    for j in range(TAPS):
        ks = [k8_ref[h, i * TAPS + j] for i in range(TAPS)]
        for p in range(rows + TAPS - 1):
            xs = [pad_col(pads, h, r0 + p, c0 + j + c) for c in range(n)]
            for q in range(max(0, p - TAPS + 1), min(rows, p + 1)):
                for c in range(n):
                    term = xs[c] * ks[p - q]
                    accs[q][c] = term if accs[q][c] is None else accs[q][c] + term
    return accs


def gelu_pair(pre):
    sq = pre * pre
    t = jnp.tanh(pre * (ROOT_TWO_PI + (ROOT_TWO_PI * CUBIC_TERM) * sq))
    half = 0.5 + 0.5 * t
    act = pre * half
    slope = half + act * (1.0 - t) * (ROOT_TWO_PI + (3.0 * ROOT_TWO_PI * CUBIC_TERM) * sq)
    return act, slope


def fold(v):
    return jnp.sum(v.reshape(v.shape[0] // 8, 8, v.shape[1]), axis=0)


def dot(a, b):
    return jnp.dot(a, b, preferred_element_type=F32)


def dot_t(a, b):
    return lax.dot_general(a, b, (((1,), (1,)), ((), ())), preferred_element_type=F32)


def dense_block(conv, x, dy, params, add_dw, add_sum):
    win, wout, bias_in, bias_out, scale, gain, shift, conv_bias = params
    hidden = win.shape[1]
    channels = win.shape[0]
    conv = conv + conv_bias[...]
    centred = conv - jnp.mean(conv, axis=1, keepdims=True)
    inv_std = lax.rsqrt(jnp.mean(centred * centred, axis=1, keepdims=True) + EPSILON)
    normed = centred * inv_std
    unit = (normed * gain[...] + shift[...]).astype(BF16)
    gb = (dy * scale[...]).astype(BF16)
    unit_t = unit.T
    gb_t = gb.T
    acts, gps = [], []
    for k in range(0, hidden, 256):
        ks = slice(k, k + 256)
        act, slope = gelu_pair(dot(unit, win[:, ks]) + bias_in[:, ks])
        gp = (dot_t(gb, wout[ks, :]) * slope).astype(BF16)
        add_sum(k // 256, fold(gp.astype(F32)))
        acts.append(act.astype(BF16))
        gps.append(gp)
    for k, act, gp in zip(range(0, hidden, 256), acts, gps):
        add_dw(0, k, dot(unit_t, gp))
        add_dw(1, k, dot(gb_t, act))
    branch = dot(jnp.concatenate(acts, axis=1), wout[...])
    grad_unit = dot_t(jnp.concatenate(gps, axis=1), win[...])
    branch = branch + bias_out[...]
    out = x + scale[...] * branch
    scaled = grad_unit * gain[...]
    grad_conv = inv_std * (
        scaled
        - jnp.mean(scaled, axis=1, keepdims=True)
        - normed * jnp.mean(scaled * normed, axis=1, keepdims=True)
    )
    grad_conv = grad_conv.astype(BF16).astype(F32)
    nk = hidden // 256
    add_sum(nk + 0, fold(gb.astype(F32)))
    add_sum(nk + 1, fold(dy * branch))
    add_sum(nk + 2, fold(grad_unit * normed))
    add_sum(nk + 3, fold(grad_unit))
    add_sum(nk + 4, fold(grad_conv))
    return out, grad_conv


def rows_of(ref, r0, nr, c0, n):
    blocks = []
    for q in range(nr):
        blocks.append(jnp.concatenate([ref[h, r0 + q, c0 * 8 : (c0 + n) * 8, :] for h in range(2)], axis=1))
    return jnp.concatenate(blocks, axis=0)


def rims_of(center_ref, nbr_ref):
    north = slot_pick(nbr_ref, 0)
    south = slot_pick(nbr_ref, 1)
    for h in range(2):
        for q in range(RIM):
            for c in range(16):
                cs = slice(c * 8, c * 8 + 8)
                center_ref[h, q, cs, :] = take(center_ref[h, 16 + q, cs, :], north)
                center_ref[h, 19 + q, cs, :] = take(center_ref[h, 3 + q, cs, :], south)


def side_rim(side_ref, halo_ref, nbr_ref, straight, up, down):
    mid, top, low = (slot_pick(nbr_ref, w) for w in (straight, up, down))
    for h in range(2):
        for pair in range(24):
            v = halo_ref[pair * 16 : pair * 16 + 16, lanes(h)].astype(F32)
            for s in range(2):
                r, c = divmod(pair * 2 + s, RIM)
                cs = slice(c * 8, c * 8 + 8)
                part = v[s * 8 : s * 8 + 8]
                side_ref[h, 3 + r, cs, :] = take(part, mid)
                if r >= 13:
                    side_ref[h, r - 13, cs, :] = take(part, top)
                if r < 3:
                    side_ref[h, 19 + r, cs, :] = take(part, low)


def inner_kernel(
    n_place, nbr_ref, cnt_ref, *refs,
):
    (x_ref, dy_ref, k_ref, win, wout, bias_in, bias_out, scale, gain, shift, conv_bias) = refs[n_place : n_place + 11]
    center_ref, dyt_ref, conv_ref, k8_ref, win_kept, wout_kept, vec_kept = refs[n_place + 11 :]
    live = cnt_ref[0]
    spread_taps(k_ref, k8_ref, False)
    win_kept[...] = win[...]
    wout_kept[...] = wout[...]
    for i, v in enumerate((bias_in, bias_out, scale, gain, shift, conv_bias)):
        vec_kept[i : i + 1, 0 : v.shape[1]] = v[...]

    def turn(r, carry):
        for t in range(8):
            for h in range(2):
                center_ref[h, 3 + r, pl.ds(t, 16, stride=8), :] = x_ref[t, r, :, lanes(h)].astype(F32)
                dyv = dy_ref[t, r, :, lanes(h)].astype(F32)
                dyt_ref[h, r, pl.ds(t, 16, stride=8), :] = jnp.where(t < live, dyv, 0.0)
        return carry

    lax.fori_loop(0, 16, turn, 0)
    rims_of(center_ref, nbr_ref)
    n, c0 = 10, 3
    pads = (None, center_ref, None)

    def conv(q, carry):
        for h in range(2):
            accs = conv_wide(pads, k8_ref, h, q, c0, n)
            conv_ref[h, q, c0 * 8 : (c0 + n) * 8, :] = jnp.concatenate(accs, axis=0)
        return carry

    lax.fori_loop(0, 16, conv, 0, unroll=2)


def edge_kernel(
    nbr_ref, hw_ref, he_ref, center_ref, dyt_ref, k8_ref, win, wout, vec,
    west_ref, east_ref, out_ref, g_ref, send_l, send_r, dw_ref, sums_ref,
    conv_ref,
):
    channels = win.shape[0]
    side_rim(west_ref, hw_ref, nbr_ref, 2, 4, 6)
    side_rim(east_ref, he_ref, nbr_ref, 3, 5, 7)
    params = (win, wout) + vectors(vec, win)
    pads = (west_ref, center_ref, east_ref)

    def add_dw(which, k, v):
        dw_ref[which * channels : (which + 1) * channels, k : k + 256] = v

    def add_sum(which, v):
        sums_ref[which] = v

    def conv(m, carry):
        r0 = m * 8
        for h in range(2):
            for side, c0 in enumerate((0, 13)):
                accs = conv_tall(pads, k8_ref, h, r0, 8, c0, RIM)
                for q in range(8):
                    at = pl.multiple_of(((r0 + q) * 2 + side) * 24, 8)
                    conv_ref[pl.ds(at, 24), lanes(h)] = jnp.concatenate(accs[q], axis=0)
        return carry

    lax.fori_loop(0, 2, conv, 0)
    xs, dys = [], []
    for q in range(16):
        for c0 in (0, 13):
            xs.append(rows_of(center_ref, 3 + q, 1, c0, RIM))
            dys.append(rows_of(dyt_ref, q, 1, c0, RIM))
    x = jnp.concatenate(xs, axis=0)
    dy = jnp.concatenate(dys, axis=0)
    out, g = dense_block(conv_ref[...], x, dy, params, add_dw, add_sum)
    for q in range(16):
        for side, c0 in enumerate((0, 13)):
            part = slice((q * 2 + side) * 24, (q * 2 + side) * 24 + 24)
            cols = slice(c0 * 8, c0 * 8 + 24)
            for h in range(2):
                out_ref[h, q, cols, :] = out[part, lanes(h)]
                g_ref[h, 3 + q, cols, :] = g[part, lanes(h)]
    for q in range(0, 16, 2):
        for side, send in enumerate((send_l, send_r)):
            v = [g[(q + s) * 48 + side * 24 : (q + s) * 48 + side * 24 + 24] for s in range(2)]
            send[q * 24 : q * 24 + 48, :] = jnp.concatenate(v, axis=0).astype(BF16)


def vectors(vec, win):
    channels, hidden = win.shape
    return tuple(vec.at[i : i + 1, 0:w] for i, w in enumerate((hidden,) + (channels,) * 5))


def middle_kernel(
    place_ref, center_ref, dyt_ref, conv_ref, dw_in, sums_in, out_in, g_in, win, wout, vec,
    out_ref, g_ref, own_ref, sent_ref, sums_ref,
    travel_ref,
):
    core = place_ref[0]
    channels, hidden = win.shape
    params = (win, wout) + vectors(vec, win)
    n, c0 = 10, 3
    cols = slice(c0 * 8, (c0 + n) * 8)

    def add_dw(which, k, v):
        v = dw_in[which * channels : (which + 1) * channels, k : k + 256] + v
        if which == 1:
            v = v.T
        v = v.astype(BF16)
        for side in range(2):
            row = k * 2 + side * 256 if which == 0 else side * hidden + k
            travel_ref[which, row : row + 256, :] = v[:, lanes(side)]

    def add_sum(which, v):
        sums_ref[which] = sums_in[which] + v

    x = rows_of(center_ref, 3, 16, c0, n)
    dy = rows_of(dyt_ref, 0, 16, c0, n)
    out, g = dense_block(rows_of(conv_ref, 0, 16, c0, n), x, dy, params, add_dw, add_sum)
    for q in range(16):
        for h in range(2):
            out_ref[h, q, cols, :] = out[q * n * 8 : (q + 1) * n * 8, lanes(h)]
            g_ref[h, 3 + q, cols, :] = g[q * n * 8 : (q + 1) * n * 8, lanes(h)]
    own_ref[...] = travel_ref[core]
    sent_ref[...] = travel_ref[1 - core]


def turn_out(out_ref, src_ref, live, r):
    for t in range(8):
        for h in range(2):
            v = src_ref[h, r, pl.ds(t, 16, stride=8), :]
            out_ref[t, r, :, lanes(h)] = jnp.where(t < live, v, 0.0).astype(BF16)


def tiles_kernel(cnt_ref, full_ref, out_ref):
    live = cnt_ref[0]

    def row(r, carry):
        turn_out(out_ref, full_ref, live, r)
        return carry

    lax.fori_loop(0, 16, row, 0)


def tap_kernel(h, first, center_ref, west_ref, east_ref, g_ref, acc_ref):
    pads = (west_ref, center_ref, east_ref)

    def row_tap(i, carry):
        def row(r, accs):
            g = [g_ref[h, 3 + r, c * 8 : c * 8 + 8, :] for c in range(16)]
            xs = [pad_col(pads, h, r + first + i, c) for c in range(22)]
            new = []
            for j in range(TAPS):
                terms = [xs[c + j] * g[c] for c in range(16)]
                while len(terms) > 1:
                    terms = [a + b for a, b in zip(terms[::2], terms[1::2])]
                new.append(accs[j] + terms[0])
            return tuple(new)

        accs = lax.fori_loop(0, 16, row, tuple(jnp.zeros((8, LANES), F32) for _ in range(TAPS)), unroll=4)
        for j in range(TAPS):
            acc_ref[i * TAPS + j] = accs[j]
        return carry

    lax.fori_loop(0, acc_ref.shape[0] // TAPS, row_tap, 0)


def sides_kernel(nbr_ref, hw_ref, he_ref, g_in, west_ref, east_ref, g_ref):
    rims_of(g_ref, nbr_ref)
    side_rim(west_ref, hw_ref, nbr_ref, 2, 4, 6)
    side_rim(east_ref, he_ref, nbr_ref, 3, 5, 7)


def back_kernel(first, last, cnt_ref, west_ref, east_ref, g_ref, dyt_ref, k_ref, *refs):
    gx_ref, full_ref, k8_ref = refs[-3:]
    live = cnt_ref[0]
    spread_taps(k_ref, k8_ref, True)
    pads = (west_ref, g_ref, east_ref)
    if len(refs) > 3:
        gx_ref[:, :first] = refs[0][...]

    def row(r, carry):
        for h in range(2):
            accs = conv_wide(pads, k8_ref, h, r, 0, 16)
            for c in range(16):
                cs = slice(c * 8, c * 8 + 8)
                full_ref[h, r, cs, :] = accs[c] + dyt_ref[h, r, cs, :]
        turn_out(gx_ref, full_ref, live, r)
        return carry

    lax.fori_loop(first, last, row, 0)


def added(held):
    total = held[0][...].astype(F32)
    for h in held[1:]:
        total = total + h[...].astype(F32)
    return total.astype(BF16)


def scatter_kernel(size, place_ref, *refs):
    held, outs = refs[:-size], refs[-size:]
    total = added(held)
    rows = total.shape[0] // size
    mine = place_ref[0]
    for p in range(size):
        piece = total[p * rows : (p + 1) * rows]
        for k in range(size):

            @pl.when((mine ^ k) == p)
            def _(k=k, piece=piece):
                outs[k][...] = piece


def finish_kernel(tap0, tap1, tap2, sums, *refs):
    held, out = refs[:-1], refs[-1]
    ns = sums.shape[0]
    total = added(held)
    rows = total.shape[0]
    out[0:rows, :] = total
    dense = jnp.sum(sums[...], axis=1)
    rest = jnp.zeros((64 - ns - 49, LANES), F32)
    for h, parts in enumerate(((tap0, tap1), (tap2,))):
        part = jnp.concatenate([dense[:, lanes(h)], *(jnp.sum(p[...], axis=1) for p in parts), rest], axis=0)
        out[rows + 64 * h : rows + 64 * h + 64, :] = part.astype(BF16)


def gather_kernel(place_ref, *refs):
    parts, out = refs[:-1], refs[-1]
    rows = parts[0].shape[0] - LANES
    mine = place_ref[0]
    total = jnp.zeros((LANES, LANES), F32)
    for k, part in enumerate(parts):
        at = mine ^ k
        out[pl.ds(pl.multiple_of(at * rows, 16), rows), :] = part[0:rows, :]
        total = total + part[rows : rows + LANES, :].astype(F32)
    out[len(parts) * rows : len(parts) * rows + LANES, :] = total.astype(BF16)


def last_kernel(
    factor, place_ref, own_ref, other_ref,
    taps_ref, conv_bias_ref, gain_ref, shift_ref, win_ref, bias_in_ref, wout_ref, bias_out_ref, scale_ref,
):
    core = place_ref[0]
    hidden = wout_ref.shape[0]
    rows = 2 * hidden

    def put_in(ref):
        for b in range(hidden // LANES):
            win_ref[:, b * LANES : (b + 1) * LANES] = ref[b * 256 : b * 256 + 256, :].astype(F32) * factor

    def put_out(ref):
        for side in range(2):
            wout_ref[:, lanes(side)] = ref[side * hidden : (side + 1) * hidden, :].astype(F32) * factor

    @pl.when(core == 0)
    def _():
        put_in(own_ref)
        put_out(other_ref)

    @pl.when(core != 0)
    def _():
        put_in(other_ref)
        put_out(own_ref)

    nk = hidden // 256
    for h in range(2):
        at = slice(rows + 64 * h, rows + 64 * h + 64)
        small = (own_ref[at, :].astype(F32) + other_ref[at, :].astype(F32)) * factor
        for k in range(nk):
            bias_in_ref[:, k * 256 + h * LANES : k * 256 + (h + 1) * LANES] = small[k : k + 1]
        for k, ref in enumerate((bias_out_ref, scale_ref, gain_ref, shift_ref, conv_bias_ref)):
            ref[:, lanes(h)] = small[nk + k : nk + k + 1]
        for i in range(TAPS):
            at = nk + 5 + i * TAPS
            taps_ref[i, :, lanes(h)] = small[at : at + TAPS]


def shifted(block, axis, distance):
    n = lax.axis_size(axis)
    return lax.ppermute(block, axis, [((i - distance) % n, i) for i in range(n)])


def crossed(v, mask):
    n = lax.axis_size(AXES)
    return lax.ppermute(v, AXES, [(i, i ^ mask) for i in range(n)])


def groups():
    total = lax.axis_size(AXES)
    found, bit = [(1, 2)], 2
    while bit < total:
        size = min(4, total // bit)
        found.append((bit, size))
        bit *= size
    return found


def on_device(
    activations, cotangent, tile_count, neighbours, conv_kernel, conv_bias, norm_gain, norm_bias,
    proj_in, bias_in, proj_out, bias_out, layer_scale,
):
    x = activations[0]
    dy = cotangent[0]
    slots, edge, _, channels = x.shape
    hidden = proj_in.shape[1]
    row = lambda v: v.reshape(1, -1)
    weights = (
        proj_in, proj_out, row(bias_in), row(bias_out), row(layer_scale), row(norm_gain), row(norm_bias),
        row(conv_bias),
    )
    weights = tuple(Far(w) for w in weights)
    conv_kernel = Far(conv_kernel)
    me = lax.axis_index(AXES)
    place = {g: ((me // g[0]) % g[1]).astype(jnp.int32).reshape(1) for g in groups()}
    neighbours = Far(neighbours)

    def columns(lo):
        return x[:, :, lo : lo + RIM].transpose(1, 2, 0, 3).reshape(edge * RIM * slots, channels)

    from_east = shifted(columns(0), "space", -1)
    from_west = shifted(columns(edge - RIM), "space", 1)
    ns = hidden // 256 + 5
    half = (2, edge, edge * slots, LANES)
    k8 = pltpu.VMEM((2, TAPS * TAPS, 8, LANES), F32)
    side = (2, edge + 2 * RIM, RIM * slots, LANES)
    tall = (2, edge + 2 * RIM, edge * slots, LANES)
    halo = (edge * RIM * slots, channels)
    sums_shape = (ns, 8, channels)
    tiles = (slots, edge, edge, channels)
    travel = (channels * hidden // LANES, LANES)
    dw_shape = (2 * channels, hidden)

    spread = (2, TAPS * TAPS, 8, LANES)
    center, dyt, conv, *kept = call(
        functools.partial(inner_kernel, len(place)),
        [(tall, F32, KEEP), (half, F32, KEEP), (half, F32, KEEP), (spread, F32, KEEP), (proj_in.shape, BF16, KEEP),
         (proj_out.shape, BF16, KEEP), ((8, hidden), F32, KEEP)],
        (neighbours, tile_count, *place.values(), Far(x), Far(dy), conv_kernel) + weights,
        smem=2 + len(place),
    )
    west, east, full, g, send_l, send_r, dw, sums = call(
        edge_kernel,
        [(side, F32, KEEP), (side, F32, KEEP), (half, F32, KEEP), (tall, F32, KEEP), (halo, BF16), (halo, BF16),
         (dw_shape, F32, KEEP), (sums_shape, F32, KEEP)],
        (neighbours, from_west, from_east, center, dyt, *kept),
        [pltpu.VMEM((edge * 2 * RIM * slots, channels), F32)],
        smem=1,
    )
    grad_from_east = shifted(send_l, "space", -1)
    grad_from_west = shifted(send_r, "space", 1)
    full, g, held, sent, sums = call(
        middle_kernel,
        [(half, F32, KEEP), (tall, F32, KEEP), (travel, BF16), (travel, BF16), (sums_shape, F32, KEEP)],
        (place[1, 2], center, dyt, conv, dw, sums, full, g, *kept[1:]),
        [pltpu.VMEM((2,) + travel, BF16)],
        smem=1,
        alias={6: 0, 7: 1},
    )
    later = groups()[1:]
    arrived = [crossed(sent, 1)]

    taps = []

    def tap(h, first, last, after):
        v, done = call(
            functools.partial(tap_kernel, h, first), [(((last - first) * TAPS, 8, LANES), F32, KEEP)],
            (center, west, east, g), after=after, token=True, work=WORK,
        )
        taps.append(v)
        return done


    *sides, g, done = call(
        sides_kernel, [(side, F32, KEEP), (side, F32, KEEP), (tall, F32, KEEP)],
        (neighbours, grad_from_west, grad_from_east, g), smem=1, alias={3: 2}, after=(tap(0, 0, 3, ()),), token=True, work=WORK,
    )
    filler = (done,)

    gx = ()
    cuts = [0, 6, 10, edge]

    def back():
        nonlocal gx
        first = gx[0].value.shape[1] if gx else 0
        last = cuts[cuts.index(first) + 1]
        *gx, done = call(
            functools.partial(back_kernel, first, last),
            [((slots, last, edge, channels), BF16, KEEP) if last < edge else (tiles, BF16)],
            (tile_count, *sides, g, dyt, conv_kernel, *gx),
            [pltpu.VMEM(half, F32), k8],
            smem=1,
            after=(begun,),
            token=True,
        )
        return done

    for n, (bit, size) in enumerate(later):
        held, *parts, begun = call(
            functools.partial(scatter_kernel, size),
            [((held.shape[0] // size, LANES), BF16)] * size,
            (place[bit, size], held, *arrived),
            smem=1,
            after=filler,
            token=True,
        )
        arrived = [crossed(p, k * bit) for k, p in enumerate(parts, 1)]
        filler = ()
        if n == 0:
            filler = (tap(0, 3, TAPS, (begun,)), tap(1, 0, TAPS, (begun,)))
        if n == 1:
            filler = (back(),)
    held, begun = call(
        finish_kernel, [((held.shape[0] + LANES, LANES), BF16)], (*taps, sums, held, *arrived), after=filler, token=True
    )

    for n, (bit, size) in enumerate(later[::-1]):
        parts = [held] + [crossed(held, k * bit) for k in range(1, size)]
        filler = (back(),) if n < 2 else ()
        rows = (held.shape[0] - LANES) * size + LANES
        held, begun = call(
            gather_kernel, [((rows, LANES), BF16)],
            (place[bit, size], *parts), smem=1, after=filler, token=True,
        )
    out_tiles, done = call(tiles_kernel, [(tiles, BF16)], (tile_count, full), smem=1, after=(begun,), token=True)
    factor = 1.0 / math.sqrt(lax.axis_size("dp") * lax.axis_size("space") * slots * edge * edge)
    vec = ((1, channels), F32)
    small = [((TAPS, TAPS, channels), F32), vec, vec, vec]
    grads = call(
        functools.partial(last_kernel, factor),
        [*small, ((channels, hidden), F32), ((1, hidden), F32), ((hidden, channels), F32), vec, vec],
        (place[1, 2], held, crossed(held, 1)),
        smem=1,
        after=(done,),
    )
    grads = [v.reshape(-1) if v.shape[0] == 1 else v for v in grads]
    return (out_tiles[None], gx[0][None], *grads)


def solution(mesh):
    tiles = P("dp", "space", None, None, None)
    return jax.shard_map(
        on_device,
        mesh=mesh,
        in_specs=(tiles, tiles, P("space"), P("space", None)) + (P(),) * 9,
        out_specs=(tiles, tiles) + (P(),) * 9,
        check_vma=False,
    )
```
